512 devices in a mesh: dp: 16 (over x_lo, y, core), fsdp: 32 (over z, x_hi).
Axes of the slice: x: 4 (x_hi: 2, x_lo: 2; x = x_hi * 2 + x_lo), y: 4, z: 16, core: 2. Of those that a mesh axis runs over, the one named last changes fastest.
Arguments:
- activations: bfloat16 [57344, 8192], P('dp', 'fsdp'), may hold values from -6 to 6
- key_grads: bfloat16 [57344, 512], P(('dp', 'fsdp')), may hold values from -0.0234375 to 0.0234375
- partners: int32 [32], replicated, may hold values from 0 to 31, each once
- master_weight: float32 [8192, 512], P('fsdp'), may hold values from -6 to 6
- first_moment: float32 [8192, 512], P('fsdp'), may hold values from -1.75 to 1.75
- second_moment: float32 [8192, 512], P('fsdp'), may hold values from 0.05 to 2
Outputs:
- new_weight: float32 [8192, 512], P('fsdp')
- new_first: float32 [8192, 512], P('fsdp')
- new_second: float32 [8192, 512], P('fsdp')
The draws below stay inside these ranges and needn't reach their ends.
Inputs may be any that keep to these rules, and one draw needn't show every extreme that they name: `partners`: each old shard index appears exactly once.
All inputs are finite; a program needn't handle non-finite values.
Results may differ from the reference program's by a relative error of at most 0.0003.
Values may be sent and summed in bfloat16 or wider, within the bound.
No kernel may reach another device: no remote copies, remote signals or barrier semaphores. Data moves between devices by JAX's collectives and lax.ppermute only.
A program may use at most 64 MiB of HBM per device.

```python
import math
import jax
import jax.numpy as jnp
from jax import lax

D = 8192
KC = 512
TOKG = 3584
TOKENS = 57344
N_DP = 16
N_FSDP = 32


def with_spikes(values, own_key, source, target, parts, factor):
    def block_of(axis_at):
        return (jnp.arange(values.shape[axis_at]) // (values.shape[axis_at] // parts)).reshape((-1,) + (1,) * (values.ndim - 1 - axis_at))

    near = jax.random.permutation(own_key, parts)[block_of(target)]
    far = (block_of(target) + parts // 2) % parts
    return jnp.where((block_of(source) == near) | (block_of(source) == far), factor * values, values)


def level_of(stream_key, extent, split, smallest, top_value):
    def one(dim, shards_of):
        heights = jax.random.uniform(jax.random.fold_in(jax.random.fold_in(stream_key, 6), dim), (shards_of,), jnp.float32, smallest / len(split), top_value / len(split))
        return jnp.repeat(jnp.exp(heights), extent[dim] // shards_of).reshape((-1,) + (1,) * (len(extent) - dim - 1))

    gain = one(*split[0])
    for cut in split[1:]:
        gain = gain * one(*cut)
    return gain


def scatter_about(key, extent, spread, bound, shards=(), dtype=jnp.bfloat16):
    level = level_of(key, extent, shards, -0.22, 0.18) if shards else 1.0
    drawn = jax.random.normal(key, extent, jnp.float32) * spread * level
    return jnp.minimum(jnp.maximum(drawn, -bound), bound).astype(dtype)


def noise_with(key, dims, scale, limit, shards, heavy, dtype=jnp.bfloat16):
    drawn = scale * jax.random.normal(key, dims, jnp.float32)
    if shards:
        drawn = drawn * level_of(key, dims, shards, -0.22, 0.18)
    return jnp.clip(with_spikes(drawn, jax.random.fold_in(key, 3), *heavy), -limit, limit).astype(dtype)


def setup_inputs(seed: int = 0) -> dict:
    streams_of = jax.random.split(jax.random.key(seed), 7)
    activations = noise_with(streams_of[0], (TOKENS, D), 1.0, 6.0, ((0, 16), (1, 32)), (0, 1, 32, 2.75))
    key_grads = scatter_about(streams_of[1], (TOKENS, KC), (1.0 / (TOKG * N_DP) ** 0.5), 0.0234375, ((0, 512),))
    partners = jax.random.permutation(streams_of[2], N_FSDP).astype(jnp.int32)
    master_weight = scatter_about(streams_of[3], (D, KC), 1.0, 6.0, ((0, 32),), jnp.float32)
    first_moment = scatter_about(streams_of[4], (D, KC), 0.3, 1.75, ((0, 32),), jnp.float32)
    second_moment = jnp.clip(jnp.exp(math.log(2.0) - 3.6888794 * jax.random.uniform(streams_of[5], (D, KC), jnp.float32) ** level_of(streams_of[5], (D, KC), ((0, 32),), -0.2, 0.2)), 0.05, 2.0)
    return {"activations": activations, "key_grads": key_grads, "partners": partners, "master_weight": master_weight, "first_moment": first_moment, "second_moment": second_moment}


beta_first = 0.9
beta_second = 0.95
learn_rate = 0.01
weight_decay = 0.1
correct_first = 1.0 - 0.9 ** 10
correct_second = 1.0 - 0.95 ** 10

def merge_rows(array, partners):
    blocks = array.reshape(N_FSDP, array.shape[0] // N_FSDP, array.shape[1])
    return jnp.take(blocks, partners.astype(jnp.int32), axis=0).reshape(array.shape)

def reference(activations, key_grads, partners, master_weight, first_moment, second_moment):
    gradient = lax.dot_general(activations, key_grads, (((0,), (0,)), ((), ())), preferred_element_type=jnp.float32)
    gradient = merge_rows(gradient, partners)
    weight = merge_rows(master_weight, partners)
    new_first = beta_first * merge_rows(first_moment, partners) + (1.0 - beta_first) * gradient
    new_second = beta_second * merge_rows(second_moment, partners) + (1.0 - beta_second) * gradient * gradient
    step_size = new_first / correct_first / (jnp.sqrt(new_second / correct_second) + 1e-08)
    new_weight = weight - learn_rate * (step_size + weight_decay * weight)
    return (new_weight, new_first, new_second)
```

```python
import jax
import jax.numpy as jnp
from jax import lax
from jax.sharding import Mesh
from jax.sharding import PartitionSpec as P

beta_first = 0.9
beta_second = 0.95
learn_rate = 0.01
weight_decay = 0.1
correct_first = 1.0 - 0.9**10
correct_second = 1.0 - 0.95**10

PARTS = (("xl", 2), ("y", 4), ("c", 2), ("z", 16), ("xh", 2))
DP = ("xl", "y", "c")
FSDP = ("z", "xh")
PLANE = ("xl", "y", "c", "xh")
SWAP = [(0, 1), (1, 0)]


def exchange(array, axes):
    return lax.all_to_all(array, axes, split_axis=0, concat_axis=0, tiled=True)


def adam_update(weight, first_moment, second_moment, gradient):
    new_first = beta_first * first_moment + (1.0 - beta_first) * gradient
    new_second = beta_second * second_moment + (1.0 - beta_second) * gradient * gradient
    step_size = new_first / correct_first / (jnp.sqrt(new_second / correct_second) + 1e-08)
    new_weight = weight - learn_rate * (step_size + weight_decay * weight)
    return (new_weight, new_first, new_second)


def on_device(activations, key_grads, partners, master_weight, first_moment, second_moment):
    mine = lax.axis_index("xh")
    other = 1 - mine
    flat = lax.axis_index(DP)

    tokens = activations.reshape(16, 2, 112, 256)
    kept = lax.dynamic_index_in_dim(tokens, mine, axis=1, keepdims=False)
    sent = lax.dynamic_index_in_dim(tokens, other, axis=1, keepdims=False)
    got = lax.ppermute(sent, "xh", SWAP)

    states = jnp.stack((master_weight, first_moment, second_moment)).reshape(3, 16, 2, 8, 512)
    rows = lax.dynamic_index_in_dim(states, flat, axis=1, keepdims=False)
    own_rows = lax.dynamic_index_in_dim(rows, mine, axis=1, keepdims=False)
    peer_rows = lax.ppermute(
        lax.dynamic_index_in_dim(rows, other, axis=1, keepdims=False), "xh", SWAP
    )

    def gather(columns):
        return lax.all_gather(columns, "z", axis=0, tiled=True)

    cotangents = (gather(key_grads[:, :256]), gather(key_grads[:, 256:]))

    def product(features):
        features = features.reshape(1792, 256)
        parts = [
            lax.dot_general(
                features, half, (((0,), (0,)), ((), ())), preferred_element_type=jnp.float32
            )
            for half in cotangents
        ]
        return jnp.concatenate(parts, axis=1)

    def by_block(own, peer):
        return jnp.where(mine == 0, own, peer), jnp.where(mine == 0, peer, own)

    low, high = by_block(product(kept), product(got))
    partial = jnp.stack((low.reshape(32, 8, 512), high.reshape(32, 8, 512)), axis=1)
    gradient = jnp.sum(exchange(partial, PLANE).reshape(32, 2, 8, 512), axis=0)

    low_rows, high_rows = by_block(own_rows, peer_rows)
    old = jnp.stack((low_rows, high_rows), axis=1)
    new = jnp.stack(adam_update(old[0], old[1], old[2], gradient))

    pieces = new.reshape(3, 2, 8, 2, 256).transpose(2, 3, 1, 0, 4).reshape(16, 12, 128)
    spread = exchange(pieces, "z").reshape(32, 6, 128)
    shuffled = jnp.take(spread, partners, axis=0).reshape(16, 12, 128)
    arrived = exchange(shuffled, "z").reshape(8, 2, 2, 3, 256)
    placed = arrived.transpose(2, 3, 0, 1, 4).reshape(1, 2, 24, 512)

    shared = jnp.broadcast_to(placed, (16, 2, 24, 512)).reshape(32, 24, 512)
    whole = exchange(shared, PLANE).reshape(32, 3, 8, 512)
    return tuple(whole[:, i].reshape(256, 512) for i in range(3))


def solution(mesh):
    names = tuple(name for name, _ in PARTS)
    sizes = tuple(size for _, size in PARTS)
    fine = Mesh(mesh.devices.reshape(sizes), names)
    return jax.shard_map(
        on_device,
        mesh=fine,
        in_specs=(
            P(DP, FSDP),
            P(DP + FSDP, None),
            P(),
            P(FSDP, None),
            P(FSDP, None),
            P(FSDP, None),
        ),
        out_specs=(P(FSDP, None), P(FSDP, None), P(FSDP, None)),
        check_vma=False,
    )
```

```python
import jax
import jax.numpy as jnp
from jax import lax
from jax.sharding import Mesh
from jax.sharding import PartitionSpec as P

beta_first = 0.9
beta_second = 0.95
learn_rate = 0.01
weight_decay = 0.1
correct_first = 1.0 - 0.9**10
correct_second = 1.0 - 0.95**10

PARTS = (("xl", 2), ("y", 4), ("c", 2), ("z", 16), ("xh", 2))
DP = ("xl", "y", "c")
FSDP = ("z", "xh")
PLANE = ("xl", "y", "c", "xh")
SWAP = [(0, 1), (1, 0)]


def exchange(array, axes):
    return lax.all_to_all(array, axes, split_axis=0, concat_axis=0, tiled=True)


def adam_update(weight, first_moment, second_moment, gradient):
    new_first = beta_first * first_moment + (1.0 - beta_first) * gradient
    new_second = beta_second * second_moment + (1.0 - beta_second) * gradient * gradient
    step_size = new_first / correct_first / (jnp.sqrt(new_second / correct_second) + 1e-08)
    new_weight = weight - learn_rate * (step_size + weight_decay * weight)
    return (new_weight, new_first, new_second)


def on_device(activations, key_grads, partners, master_weight, first_moment, second_moment):
    mine = lax.axis_index("xh")
    other = 1 - mine
    flat = lax.axis_index(DP)

    tokens = activations.reshape(16, 2, 112, 256)
    kept = lax.dynamic_index_in_dim(tokens, mine, axis=1, keepdims=False)
    sent = lax.dynamic_index_in_dim(tokens, other, axis=1, keepdims=False)
    got = lax.ppermute(sent, "xh", SWAP)

    row = 16 * flat
    rows = jnp.stack(
        [
            lax.dynamic_slice_in_dim(item, row, 16, axis=0)
            for item in (master_weight, first_moment, second_moment)
        ]
    )
    along = lax.all_gather(rows, "z", axis=0, tiled=False)
    def gather(columns):
        return lax.all_gather(columns, "z", axis=0, tiled=True)

    cotangents = (gather(key_grads[:, :256]), gather(key_grads[:, 256:]))

    def product(features):
        features = features.reshape(1792, 256)
        parts = [
            lax.dot_general(
                features, half, (((0,), (0,)), ((), ())), preferred_element_type=jnp.float32
            )
            for half in cotangents
        ]
        return jnp.concatenate(parts, axis=1)

    def by_block(own, peer):
        return jnp.where(mine == 0, own, peer), jnp.where(mine == 0, peer, own)

    low, high = by_block(product(kept), product(got))
    partial = jnp.stack((low.reshape(32, 8, 512), high.reshape(32, 8, 512)), axis=1)
    along, partial = lax.optimization_barrier((along, partial))
    here = 2 * lax.axis_index("z")
    wanted = partners[here + mine]
    wanted_there = partners[here + other]
    from_here = lax.dynamic_index_in_dim(along, wanted // 2, axis=0, keepdims=False)
    for_there = lax.dynamic_index_in_dim(along, wanted_there // 2, axis=0, keepdims=False)
    from_there = lax.ppermute(for_there, "xh", SWAP)
    picked = jnp.where(wanted % 2 == mine, from_here, from_there)
    states = lax.all_gather(picked, DP, axis=0, tiled=False)
    weight, moment_one, moment_two = (states[:, i].reshape(256, 512) for i in range(3))

    gradient = jnp.sum(exchange(partial, PLANE).reshape(32, 2, 8, 512), axis=0)

    blocks = lax.all_gather(gradient, "z", axis=0, tiled=True)
    placed = jnp.stack(
        [
            lax.dynamic_index_in_dim(blocks, partners[here + i], axis=0, keepdims=False)
            for i in range(2)
        ]
    )
    shared = jnp.broadcast_to(placed[None], (16, 2, 8, 512)).reshape(32, 8, 512)
    merged = exchange(shared, PLANE).reshape(256, 512)
    return adam_update(weight, moment_one, moment_two, merged)


def solution(mesh):
    names = tuple(name for name, _ in PARTS)
    sizes = tuple(size for _, size in PARTS)
    fine = Mesh(mesh.devices.reshape(sizes), names)
    return jax.shard_map(
        on_device,
        mesh=fine,
        in_specs=(
            P(DP, FSDP),
            P(DP + FSDP, None),
            P(),
            P(FSDP, None),
            P(FSDP, None),
            P(FSDP, None),
        ),
        out_specs=(P(FSDP, None), P(FSDP, None), P(FSDP, None)),
        check_vma=False,
    )
```

```python
import jax
import jax.numpy as jnp
from jax import lax
from jax.sharding import Mesh
from jax.sharding import PartitionSpec as P

beta_first = 0.9
beta_second = 0.95
learn_rate = 0.01
weight_decay = 0.1
correct_first = 1.0 - 0.9**10
correct_second = 1.0 - 0.95**10

PARTS = (("xl", 2), ("y", 4), ("c", 2), ("z", 16), ("xh", 2))
DP = ("xl", "y", "c")
FSDP = ("z", "xh")
CHIPS = ("xl", "y", "xh")
SWAP = [(0, 1), (1, 0)]
KEY_SCALE = 2.0**21
REST_SCALE = 2.0**11
SECOND_SCALE = 2.0**-6


def exchange(array):
    return lax.all_to_all(array, CHIPS, split_axis=0, concat_axis=0, tiled=True)


def pick(array, index, axis):
    return lax.dynamic_index_in_dim(array, index, axis=axis, keepdims=False)


def split_halves(values):
    high = lax.reduce_precision(values, exponent_bits=5, mantissa_bits=10)
    rest = (values - high) * REST_SCALE
    return jnp.stack((high.astype(jnp.float16), rest.astype(jnp.float16)))


def join_halves(halves):
    wide = halves.astype(jnp.float32)
    return wide[0] + wide[1] * (1.0 / REST_SCALE)


def adam_update(weight, first_moment, second_moment, gradient):
    new_first = beta_first * first_moment + (1.0 - beta_first) * gradient
    new_second = beta_second * second_moment + (1.0 - beta_second) * gradient * gradient
    step_size = new_first / correct_first / (jnp.sqrt(new_second / correct_second) + 1e-08)
    new_weight = weight - learn_rate * (step_size + weight_decay * weight)
    return (new_weight, new_first, new_second)


def on_device(activations, key_grads, partners, master_weight, first_moment, second_moment):
    mine = lax.axis_index("xh")
    other = 1 - mine
    core = lax.axis_index("c")
    column = lax.axis_index(("xl", "y"))

    def by_block(own, peer):
        return jnp.where(mine == 0, own, peer), jnp.where(mine == 0, peer, own)

    tokens = activations.reshape(16, 2, 112, 256)
    kept = pick(tokens, mine, 1)
    got = lax.ppermute(pick(tokens, other, 1), "xh", SWAP)

    first_row = 128 * core + 16 * column

    def eight(side):
        return jnp.stack(
            [
                lax.dynamic_slice_in_dim(item, first_row + 8 * side, 8, axis=0)
                for item in (master_weight, first_moment, second_moment)
            ]
        )

    own_rows = eight(mine)
    peer_rows = lax.ppermute(eight(other), "xh", SWAP)

    scaled = (key_grads.astype(jnp.float32) * KEY_SCALE).astype(jnp.float16)
    cotangents = lax.all_gather(scaled, "z", axis=0, tiled=True)
    cotangents, got, peer_rows = lax.optimization_barrier((cotangents, got, peer_rows))
    cotangents = (cotangents.astype(jnp.float32) * (1.0 / KEY_SCALE)).astype(jnp.bfloat16)

    def product(features):
        return lax.dot_general(
            features.reshape(1792, 256),
            cotangents,
            (((0,), (0,)), ((), ())),
            preferred_element_type=jnp.float32,
        ).reshape(2, 16, 8, 512)

    partial = jnp.stack(by_block(product(kept), product(got)), axis=2)
    summed = pick(partial, core, 0) + lax.ppermute(pick(partial, 1 - core, 0), "c", SWAP)
    gradient = jnp.sum(exchange(summed), axis=0)

    old = jnp.stack(by_block(own_rows, peer_rows), axis=1)
    weight, moment_one, moment_two = adam_update(old[0], old[1], old[2], gradient)

    slices = jnp.stack((weight, moment_one, moment_two * SECOND_SCALE), axis=1)
    along = lax.all_gather(split_halves(slices), "z", axis=0, tiled=False)
    here = 2 * lax.axis_index("z")

    def wanted(index):
        place = partners[index]
        return join_halves(pick(pick(along, place // 2, 0), place % 2, 1))

    placed = jnp.stack([wanted(here + i) for i in range(2)]).reshape(1, 2, 3, 8, 512)
    half = exchange(jnp.broadcast_to(placed, (8, 2, 3, 8, 512)).reshape(16, 3, 8, 512))
    sibling = lax.ppermute(half, "c", SWAP)
    lower = jnp.where(core == 0, half, sibling)
    upper = jnp.where(core == 0, sibling, half)

    def whole(i):
        return jnp.concatenate(
            (lower[:, i].reshape(128, 512), upper[:, i].reshape(128, 512)), axis=0
        )

    return whole(0), whole(1), whole(2) * (1.0 / SECOND_SCALE)


def solution(mesh):
    names = tuple(name for name, _ in PARTS)
    sizes = tuple(size for _, size in PARTS)
    fine = Mesh(mesh.devices.reshape(sizes), names)
    return jax.shard_map(
        on_device,
        mesh=fine,
        in_specs=(
            P(DP, FSDP),
            P(DP + FSDP, None),
            P(),
            P(FSDP, None),
            P(FSDP, None),
            P(FSDP, None),
        ),
        out_specs=(P(FSDP, None), P(FSDP, None), P(FSDP, None)),
        check_vma=False,
    )
```

```python
import jax
import jax.numpy as jnp
from jax import lax
from jax.sharding import Mesh
from jax.sharding import PartitionSpec as P

beta_first = 0.9
beta_second = 0.95
learn_rate = 0.01
weight_decay = 0.1
correct_first = 1.0 - 0.9**10
correct_second = 1.0 - 0.95**10

PARTS = (("xl", 2), ("y", 4), ("c", 2), ("z", 16), ("xh", 2))
DP = ("xl", "y", "c")
FSDP = ("z", "xh")
CHIPS = ("xl", "y", "xh")
PLANE = ("c", "xl", "y", "xh")
SWAP = [(0, 1), (1, 0)]
KEY_SCALE = 2.0**21
REST_SCALE = 2.0**11
SECOND_SCALE = 2.0**-6
PARTIAL_SCALE = 2.0**7


def exchange(array, axes):
    return lax.all_to_all(array, axes, split_axis=0, concat_axis=0, tiled=True)


def pick(array, index, axis):
    return lax.dynamic_index_in_dim(array, index, axis=axis, keepdims=False)


def split_halves(values):
    high = lax.reduce_precision(values, exponent_bits=5, mantissa_bits=10)
    rest = (values - high) * REST_SCALE
    return jnp.stack((high.astype(jnp.float16), rest.astype(jnp.float16)))


def join_halves(halves):
    wide = halves.astype(jnp.float32)
    return wide[0] + wide[1] * (1.0 / REST_SCALE)


def adam_update(weight, first_moment, second_moment, gradient):
    new_first = beta_first * first_moment + (1.0 - beta_first) * gradient
    new_second = beta_second * second_moment + (1.0 - beta_second) * gradient * gradient
    step_size = new_first / correct_first / (jnp.sqrt(new_second / correct_second) + 1e-08)
    new_weight = weight - learn_rate * (step_size + weight_decay * weight)
    return (new_weight, new_first, new_second)


def on_device(activations, key_grads, partners, master_weight, first_moment, second_moment):
    mine = lax.axis_index("xh")
    other = 1 - mine
    core = lax.axis_index("c")
    column = lax.axis_index(("xl", "y"))

    def by_block(own, peer):
        return jnp.where(mine == 0, own, peer), jnp.where(mine == 0, peer, own)

    tokens = activations.reshape(16, 2, 112, 256)
    got = lax.ppermute(pick(tokens, other, 1), "xh", SWAP)

    first_row = 128 * core + 16 * column

    def eight(side):
        return jnp.stack(
            [
                lax.dynamic_slice_in_dim(item, first_row + 8 * side, 8, axis=0)
                for item in (master_weight, first_moment, second_moment)
            ]
        )

    own_rows = eight(mine)
    peer_rows = lax.ppermute(eight(other), "xh", SWAP)

    scaled = (key_grads.astype(jnp.float32) * KEY_SCALE).astype(jnp.float16)
    cotangents = lax.all_gather(scaled, "z", axis=0, tiled=True)
    cotangents, got, peer_rows, tokens = lax.optimization_barrier(
        (cotangents, got, peer_rows, tokens)
    )
    kept = pick(tokens, mine, 1)
    cotangents = (cotangents.astype(jnp.float32) * (1.0 / KEY_SCALE)).astype(jnp.bfloat16)

    def product(features):
        return lax.dot_general(
            features.reshape(1792, 256),
            cotangents,
            (((0,), (0,)), ((), ())),
            preferred_element_type=jnp.float32,
        ).reshape(32, 8, 512)

    partial = jnp.stack(by_block(product(kept), product(got)), axis=1)
    pieces = exchange((partial * PARTIAL_SCALE).astype(jnp.float16), PLANE)
    gradient = jnp.sum(pieces.astype(jnp.float32), axis=0) * (1.0 / PARTIAL_SCALE)

    old = jnp.stack(by_block(own_rows, peer_rows), axis=1)
    weight, moment_one, moment_two = adam_update(old[0], old[1], old[2], gradient)

    slices = jnp.stack((weight, moment_one, moment_two * SECOND_SCALE), axis=1)
    along = lax.all_gather(split_halves(slices), "z", axis=0, tiled=False)
    here = 2 * lax.axis_index("z")

    def wanted(index):
        place = partners[index]
        return join_halves(pick(pick(along, place // 2, 0), place % 2, 1))

    placed = jnp.stack([wanted(here + i) for i in range(2)]).reshape(1, 2, 3, 8, 512)
    half = exchange(jnp.broadcast_to(placed, (8, 2, 3, 8, 512)).reshape(16, 3, 8, 512), CHIPS)
    sibling = lax.ppermute(half, "c", SWAP)
    lower = jnp.where(core == 0, half, sibling)
    upper = jnp.where(core == 0, sibling, half)

    def whole(i):
        return jnp.concatenate(
            (lower[:, i].reshape(128, 512), upper[:, i].reshape(128, 512)), axis=0
        )

    return whole(0), whole(1), whole(2) * (1.0 / SECOND_SCALE)


def solution(mesh):
    names = tuple(name for name, _ in PARTS)
    sizes = tuple(size for _, size in PARTS)
    fine = Mesh(mesh.devices.reshape(sizes), names)
    return jax.shard_map(
        on_device,
        mesh=fine,
        in_specs=(
            P(DP, FSDP),
            P(DP + FSDP, None),
            P(),
            P(FSDP, None),
            P(FSDP, None),
            P(FSDP, None),
        ),
        out_specs=(P(FSDP, None), P(FSDP, None), P(FSDP, None)),
        check_vma=False,
    )
```

```python
import jax
import jax.numpy as jnp
from jax import lax
from jax.experimental import pallas as pl
from jax.experimental.pallas import tpu as pltpu
from jax.sharding import Mesh
from jax.sharding import PartitionSpec as P

beta_first = 0.9
beta_second = 0.95
learn_rate = 0.01
weight_decay = 0.1
correct_first = 1.0 - 0.9**10
correct_second = 1.0 - 0.95**10

PARTS = (("xl", 2), ("y", 4), ("c", 2), ("z", 16), ("xh", 2))
DP = ("xl", "y", "c")
FSDP = ("z", "xh")
CHIPS = ("xl", "y", "xh")
PLANE = ("c", "xl", "y", "xh")
SWAP = [(0, 1), (1, 0)]
KEY_SCALE = 2.0**21
REST_SCALE = 2.0**11
SECOND_SCALE = 2.0**-6
PARTIAL_SCALE = 2.0**7


def exchange(array, axes):
    return lax.all_to_all(array, axes, split_axis=0, concat_axis=0, tiled=True)


def pick(array, index, axis):
    return lax.dynamic_index_in_dim(
        array, index, axis=axis, keepdims=False, allow_negative_indices=False
    )


def split_halves(values):
    high = lax.reduce_precision(values, exponent_bits=5, mantissa_bits=10)
    rest = (values - high) * REST_SCALE
    return jnp.stack((high.astype(jnp.float16), rest.astype(jnp.float16)))


def join_halves(halves):
    wide = halves.astype(jnp.float32)
    return wide[0] + wide[1] * (1.0 / REST_SCALE)


def adam_update(weight, first_moment, second_moment, gradient):
    new_first = beta_first * first_moment + (1.0 - beta_first) * gradient
    new_second = beta_second * second_moment + (1.0 - beta_second) * gradient * gradient
    step_size = new_first / correct_first / (jnp.sqrt(new_second / correct_second) + 1e-08)
    new_weight = weight - learn_rate * (step_size + weight_decay * weight)
    return (new_weight, new_first, new_second)


def products_kernel(mine_ref, tokens_ref, got_ref, cotangents_ref, out_ref, kept, arrived):
    mine = mine_ref[0]
    fetch = pltpu.make_async_copy(tokens_ref.at[:, mine], kept, arrived)
    fetch.start()

    def product(features):
        return lax.dot_general(
            features,
            cotangents_ref[...],
            (((0,), (0,)), ((), ())),
            preferred_element_type=jnp.float32,
        ).reshape(32, 8, 512)

    out_ref[:, 1 - mine] = product(got_ref[...])
    fetch.wait()
    out_ref[:, mine] = product(kept[...].reshape(1792, 256))


def products(mine, tokens, got, cotangents):
    in_vmem = pl.BlockSpec(memory_space=pltpu.VMEM)
    return pl.pallas_call(
        products_kernel,
        out_shape=jax.ShapeDtypeStruct((32, 2, 8, 512), jnp.float32),
        in_specs=[
            pl.BlockSpec(memory_space=pltpu.SMEM),
            pl.BlockSpec(memory_space=pl.ANY),
            in_vmem,
            in_vmem,
        ],
        out_specs=in_vmem,
        scratch_shapes=[
            pltpu.VMEM((16, 112, 256), jnp.bfloat16),
            pltpu.SemaphoreType.DMA,
        ],
        compiler_params=pltpu.CompilerParams(vmem_limit_bytes=40 * 1024 * 1024),
        cost_estimate=pl.CostEstimate(
            flops=2 * 2 * 1792 * 256 * 512, bytes_accessed=6 * 1024 * 1024, transcendentals=0
        ),
    )(mine.reshape(1), tokens, got, cotangents)


def assemble_kernel(core_ref, half_ref, sibling_ref, *refs):
    outs, done = refs[:3], refs[3]
    core = core_ref[0]
    copies = []
    for i in range(3):
        for j, (source, place) in enumerate(((half_ref, core), (sibling_ref, 1 - core))):
            copies.append(
                pltpu.make_async_copy(source.at[:, i], outs[i].at[place], done.at[2 * i + j])
            )
    for copy in copies:
        copy.start()
    for copy in copies:
        copy.wait()


def assemble(core, half, sibling):
    in_vmem = pl.BlockSpec(memory_space=pltpu.VMEM)
    outs = pl.pallas_call(
        assemble_kernel,
        out_shape=[jax.ShapeDtypeStruct((2, 16, 8, 512), jnp.float32)] * 3,
        in_specs=[pl.BlockSpec(memory_space=pltpu.SMEM), in_vmem, in_vmem],
        out_specs=[pl.BlockSpec(memory_space=pl.ANY)] * 3,
        scratch_shapes=[pltpu.SemaphoreType.DMA((6,))],
        compiler_params=pltpu.CompilerParams(vmem_limit_bytes=40 * 1024 * 1024),
    )(core.reshape(1), half, sibling)
    return tuple(item.reshape(256, 512) for item in outs)


def on_device(activations, key_grads, partners, master_weight, first_moment, second_moment):
    mine = lax.axis_index("xh")
    other = 1 - mine
    core = lax.axis_index("c")
    column = lax.axis_index(("xl", "y"))

    def by_block(own, peer):
        return jnp.where(mine == 0, own, peer), jnp.where(mine == 0, peer, own)

    tokens = activations.reshape(16, 2, 112, 256)
    got = lax.ppermute(pick(tokens, other, 1), "xh", SWAP)

    first_row = 128 * core + 16 * column

    def eight(side):
        return jnp.stack(
            [
                lax.dynamic_slice_in_dim(
                    item, first_row + 8 * side, 8, axis=0, allow_negative_indices=False
                )
                for item in (master_weight, first_moment, second_moment)
            ]
        )

    scaled = (key_grads.astype(jnp.float32) * KEY_SCALE).astype(jnp.float16)
    cotangents = lax.all_gather(scaled, "z", axis=0, tiled=True)
    own_rows, outgoing, cotangents = lax.optimization_barrier(
        (eight(mine), eight(other), cotangents)
    )
    peer_rows = lax.ppermute(outgoing, "xh", SWAP)
    cotangents = (cotangents.astype(jnp.float32) * (1.0 / KEY_SCALE)).astype(jnp.bfloat16)

    partial = products(mine, tokens, got.reshape(1792, 256), cotangents)
    pieces = exchange((partial * PARTIAL_SCALE).astype(jnp.float16), PLANE)
    gradient = jnp.sum(pieces.astype(jnp.float32), axis=0) * (1.0 / PARTIAL_SCALE)

    old = jnp.stack(by_block(own_rows, peer_rows), axis=1)
    weight, moment_one, moment_two = adam_update(old[0], old[1], old[2], gradient)

    slices = jnp.stack((weight, moment_one, moment_two * SECOND_SCALE), axis=1)
    along = lax.all_gather(split_halves(slices), "z", axis=0, tiled=False)
    here = 2 * lax.axis_index("z")

    scales = jnp.array([1.0, 1.0, 1.0 / SECOND_SCALE], jnp.float32).reshape(3, 1, 1)

    def wanted(index):
        place = pick(partners, index, 0)
        return join_halves(pick(pick(along, place >> 1, 0), place & 1, 1)) * scales

    placed = jnp.stack([wanted(here + i) for i in range(2)]).reshape(1, 2, 3, 8, 512)
    half = exchange(jnp.broadcast_to(placed, (8, 2, 3, 8, 512)).reshape(16, 3, 8, 512), CHIPS)
    sibling = lax.ppermute(half, "c", SWAP)
    return assemble(core, half, sibling)


def solution(mesh):
    names = tuple(name for name, _ in PARTS)
    sizes = tuple(size for _, size in PARTS)
    fine = Mesh(mesh.devices.reshape(sizes), names)
    return jax.shard_map(
        on_device,
        mesh=fine,
        in_specs=(
            P(DP, FSDP),
            P(DP + FSDP, None),
            P(),
            P(FSDP, None),
            P(FSDP, None),
            P(FSDP, None),
        ),
        out_specs=(P(FSDP, None), P(FSDP, None), P(FSDP, None)),
        check_vma=False,
    )
```

```python
import jax
import jax.numpy as jnp
from jax import lax
from jax.experimental import pallas as pl
from jax.experimental.pallas import tpu as pltpu
from jax.sharding import Mesh
from jax.sharding import PartitionSpec as P

beta_first = 0.9
beta_second = 0.95
learn_rate = 0.01
weight_decay = 0.1
correct_first = 1.0 - 0.9**10
correct_second = 1.0 - 0.95**10

PARTS = (("xl", 2), ("y", 4), ("c", 2), ("z", 16), ("xh", 2))
DP = ("xl", "y", "c")
FSDP = ("z", "xh")
CHIPS = ("xl", "y", "xh")
PLANE = ("c", "xl", "y", "xh")
SWAP = [(0, 1), (1, 0)]
KEY_SCALE = 2.0**21
REST_SCALE = 2.0**11
SECOND_SCALE = 2.0**-6
PARTIAL_SCALE = 2.0**7


def exchange(array, axes):
    return lax.all_to_all(array, axes, split_axis=0, concat_axis=0, tiled=True)


def pick(array, index, axis):
    return lax.dynamic_index_in_dim(
        array, index, axis=axis, keepdims=False, allow_negative_indices=False
    )


def split_halves(values):
    high = lax.reduce_precision(values, exponent_bits=5, mantissa_bits=10)
    rest = (values - high) * REST_SCALE
    return jnp.stack((high.astype(jnp.float16), rest.astype(jnp.float16)), axis=1)


def join_halves(halves):
    wide = halves.astype(jnp.float32)
    return wide[0] + wide[1] * (1.0 / REST_SCALE)


def adam_update(weight, first_moment, second_moment, gradient):
    new_first = beta_first * first_moment + (1.0 - beta_first) * gradient
    new_second = beta_second * second_moment + (1.0 - beta_second) * gradient * gradient
    step_size = new_first / correct_first / (jnp.sqrt(new_second / correct_second) + 1e-08)
    new_weight = weight - learn_rate * (step_size + weight_decay * weight)
    return (new_weight, new_first, new_second)


def message_kernel(
    where_ref, tokens_ref, weight_ref, one_ref, two_ref, out_ref, rows, tail, sent, read, last
):
    other, row = where_ref[0], pl.multiple_of(where_ref[1], 8)
    copies = [pltpu.make_async_copy(tokens_ref.at[:, other], out_ref.at[pl.ds(0, 16)], sent)]
    for i, state_ref in enumerate((weight_ref, one_ref, two_ref)):
        copies.append(
            pltpu.make_async_copy(state_ref.at[pl.ds(row, 8)], rows.at[i], read.at[i])
        )
    for copy in copies:
        copy.start()
    for copy in copies[1:]:
        copy.wait()
    values = rows[...].reshape(24, 512)
    values = jnp.concatenate((values[:, :256], values[:, 256:]), axis=0)
    first = values.astype(jnp.bfloat16)
    values = values - first.astype(jnp.float32)
    second = values.astype(jnp.bfloat16)
    third = (values - second.astype(jnp.float32)).astype(jnp.bfloat16)
    tail[0, 0:48] = first
    tail[0, 48:96] = second
    tail[0, 96:112] = jnp.zeros((16, 256), jnp.bfloat16)
    tail[1, 0:48] = third
    tail[1, 48:112] = jnp.zeros((64, 256), jnp.bfloat16)
    end = pltpu.make_async_copy(tail, out_ref.at[pl.ds(16, 2)], last)
    end.start()
    copies[0].wait()
    end.wait()


def message(other, row, tokens, states):
    return pl.pallas_call(
        message_kernel,
        out_shape=jax.ShapeDtypeStruct((18, 112, 256), jnp.bfloat16),
        in_specs=[pl.BlockSpec(memory_space=pltpu.SMEM)]
        + [pl.BlockSpec(memory_space=pltpu.HBM)] * 4,
        out_specs=pl.BlockSpec(memory_space=pltpu.HBM),
        scratch_shapes=[
            pltpu.VMEM((3, 8, 512), jnp.float32),
            pltpu.VMEM((2, 112, 256), jnp.bfloat16),
            pltpu.SemaphoreType.DMA,
            pltpu.SemaphoreType.DMA((3,)),
            pltpu.SemaphoreType.DMA,
        ],
        compiler_params=pltpu.CompilerParams(vmem_limit_bytes=60 * 1024 * 1024),
    )(jnp.stack((other, row)), tokens, *states)


def products_kernel(
    mine_ref, tokens_ref, got_ref, cotangents_ref, out_ref, rows_ref, kept, arrived
):
    mine = mine_ref[0]
    fetch = pltpu.make_async_copy(tokens_ref.at[:, mine], kept, arrived)
    fetch.start()

    def product(features):
        return lax.dot_general(
            features,
            cotangents_ref[...],
            (((0,), (0,)), ((), ())),
            preferred_element_type=jnp.float32,
        ).reshape(32, 8, 512)

    out_ref[:, 1 - mine] = product(got_ref[0:16].reshape(1792, 256))
    rows = (
        got_ref[16, 0:48].astype(jnp.float32) + got_ref[16, 48:96].astype(jnp.float32)
    ) + got_ref[17, 0:48].astype(jnp.float32)
    rows_ref[...] = jnp.concatenate((rows[:24], rows[24:]), axis=1).reshape(3, 8, 512)
    fetch.wait()
    out_ref[:, mine] = product(kept[...].reshape(1792, 256))


def products(mine, tokens, got, cotangents):
    in_vmem = pl.BlockSpec(memory_space=pltpu.VMEM)
    return pl.pallas_call(
        products_kernel,
        out_shape=[
            jax.ShapeDtypeStruct((32, 2, 8, 512), jnp.float32),
            jax.ShapeDtypeStruct((3, 8, 512), jnp.float32),
        ],
        in_specs=[
            pl.BlockSpec(memory_space=pltpu.SMEM),
            pl.BlockSpec(memory_space=pltpu.HBM),
            in_vmem,
            in_vmem,
        ],
        out_specs=[in_vmem, in_vmem],
        scratch_shapes=[
            pltpu.VMEM((16, 112, 256), jnp.bfloat16),
            pltpu.SemaphoreType.DMA,
        ],
        compiler_params=pltpu.CompilerParams(vmem_limit_bytes=40 * 1024 * 1024),
        cost_estimate=pl.CostEstimate(
            flops=2 * 2 * 1792 * 256 * 512, bytes_accessed=6 * 1024 * 1024, transcendentals=0
        ),
    )(mine.reshape(1), tokens, got, cotangents)


def assemble_kernel(core_ref, half_ref, sibling_ref, *refs):
    outs, done = refs[:3], refs[3]
    core = core_ref[0]
    copies = []
    for i in range(3):
        for j, (source, place) in enumerate(((half_ref, core), (sibling_ref, 1 - core))):
            copies.append(
                pltpu.make_async_copy(source.at[:, i], outs[i].at[place], done.at[2 * i + j])
            )
    for copy in copies:
        copy.start()
    for copy in copies:
        copy.wait()


def assemble(core, half, sibling):
    in_vmem = pl.BlockSpec(memory_space=pltpu.VMEM)
    outs = pl.pallas_call(
        assemble_kernel,
        out_shape=[jax.ShapeDtypeStruct((2, 16, 8, 512), jnp.float32)] * 3,
        in_specs=[pl.BlockSpec(memory_space=pltpu.SMEM), in_vmem, in_vmem],
        out_specs=[pl.BlockSpec(memory_space=pltpu.HBM)] * 3,
        scratch_shapes=[pltpu.SemaphoreType.DMA((6,))],
        compiler_params=pltpu.CompilerParams(vmem_limit_bytes=40 * 1024 * 1024),
    )(core.reshape(1), half, sibling)
    return tuple(item.reshape(256, 512) for item in outs)


def on_device(activations, key_grads, partners, master_weight, first_moment, second_moment):
    mine = lax.axis_index("xh")
    other = 1 - mine
    core = lax.axis_index("c")
    column = lax.axis_index(("xl", "y"))

    def by_block(own, peer):
        return jnp.where(mine == 0, own, peer), jnp.where(mine == 0, peer, own)

    states = (master_weight, first_moment, second_moment)
    first_row = 128 * core + 16 * column
    tokens = activations.reshape(16, 2, 112, 256)
    got = lax.ppermute(message(other, first_row + 8 * other, tokens, states), "xh", SWAP)

    scaled = (key_grads.astype(jnp.float32) * KEY_SCALE).astype(jnp.float16)
    cotangents = lax.all_gather(scaled, "z", axis=0, tiled=True)
    cotangents = (cotangents.astype(jnp.float32) * (1.0 / KEY_SCALE)).astype(jnp.bfloat16)

    partial, peer_rows = products(mine, tokens, got, cotangents)
    states, partial = lax.optimization_barrier((states, partial))
    own_rows = jnp.stack(
        [
            lax.dynamic_slice_in_dim(
                item, first_row + 8 * mine, 8, axis=0, allow_negative_indices=False
            )
            for item in states
        ]
    )
    pieces = exchange((partial * PARTIAL_SCALE).astype(jnp.float16), PLANE)
    gradient = jnp.sum(pieces.astype(jnp.float32), axis=0) * (1.0 / PARTIAL_SCALE)

    old = jnp.stack(by_block(own_rows, peer_rows), axis=1)
    weight, moment_one, moment_two = adam_update(old[0], old[1], old[2], gradient)

    slices = jnp.stack((weight, moment_one, moment_two * SECOND_SCALE), axis=1)
    along = lax.all_gather(split_halves(slices).reshape(2, 48, 512), "z", axis=0)
    along = along.reshape(32, 2, 3, 8, 512)
    here = 2 * lax.axis_index("z")

    scales = jnp.where(jnp.arange(3) == 2, 1.0 / SECOND_SCALE, 1.0).reshape(3, 1, 1)

    def wanted(index):
        return join_halves(pick(along, pick(partners, index, 0), 0)) * scales

    placed = jnp.stack([wanted(here + i) for i in range(2)]).reshape(1, 2, 3, 8, 512)
    half = exchange(jnp.broadcast_to(placed, (8, 2, 3, 8, 512)).reshape(16, 3, 8, 512), CHIPS)
    sibling = lax.ppermute(half, "c", SWAP)
    return assemble(core, half, sibling)


def solution(mesh):
    names = tuple(name for name, _ in PARTS)
    sizes = tuple(size for _, size in PARTS)
    fine = Mesh(mesh.devices.reshape(sizes), names)
    return jax.shard_map(
        on_device,
        mesh=fine,
        in_specs=(
            P(DP, FSDP),
            P(DP + FSDP, None),
            P(),
            P(FSDP, None),
            P(FSDP, None),
            P(FSDP, None),
        ),
        out_specs=(P(FSDP, None), P(FSDP, None), P(FSDP, None)),
        check_vma=False,
    )
```

```python
import jax
import jax.numpy as jnp
from jax import lax
from jax.experimental import pallas as pl
from jax.experimental.pallas import tpu as pltpu
from jax.sharding import Mesh
from jax.sharding import PartitionSpec as P

beta_first = 0.9
beta_second = 0.95
learn_rate = 0.01
weight_decay = 0.1
correct_first = 1.0 - 0.9**10
correct_second = 1.0 - 0.95**10

PARTS = (("xl", 2), ("y", 4), ("c", 2), ("z", 16), ("xh", 2))
DP = ("xl", "y", "c")
FSDP = ("z", "xh")
CHIPS = ("xl", "y", "xh")
SWAP = [(0, 1), (1, 0)]
KEY_SCALE = 2.0**21
REST_SCALE = 2.0**11
SECOND_SCALE = 2.0**-6
PARTIAL_SCALE = 2.0**6


def exchange(array, axes):
    return lax.all_to_all(array, axes, split_axis=0, concat_axis=0, tiled=True)


def pick(array, index, axis):
    return lax.dynamic_index_in_dim(
        array, index, axis=axis, keepdims=False, allow_negative_indices=False
    )


def split_halves(values):
    high = lax.reduce_precision(values, exponent_bits=5, mantissa_bits=10)
    rest = (values - high) * REST_SCALE
    return jnp.stack((high.astype(jnp.float16), rest.astype(jnp.float16)), axis=1)


def join_halves(halves):
    wide = halves.astype(jnp.float32)
    return wide[0] + wide[1] * (1.0 / REST_SCALE)


def adam_update(weight, first_moment, second_moment, gradient):
    new_first = beta_first * first_moment + (1.0 - beta_first) * gradient
    new_second = beta_second * second_moment + (1.0 - beta_second) * gradient * gradient
    step_size = new_first / correct_first / (jnp.sqrt(new_second / correct_second) + 1e-08)
    new_weight = weight - learn_rate * (step_size + weight_decay * weight)
    return (new_weight, new_first, new_second)


def products_kernel(where_ref, tokens_ref, got_ref, cotangents_ref, out_ref, kept, arrived):
    mine = where_ref[0]
    features = pl.ds(pl.multiple_of(128 * where_ref[1], 128), 128)
    fetch = pltpu.make_async_copy(tokens_ref.at[:, mine, :, features], kept, arrived)
    fetch.start()

    def product(block):
        return lax.dot_general(
            block,
            cotangents_ref[...],
            (((0,), (0,)), ((), ())),
            preferred_element_type=jnp.float32,
        ).reshape(16, 8, 512)

    out_ref[:, 1 - mine] = product(got_ref[:, features])
    fetch.wait()
    out_ref[:, mine] = product(kept[...].reshape(1792, 128))


def products(mine, half, tokens, got, cotangents):
    in_vmem = pl.BlockSpec(memory_space=pltpu.VMEM)
    return pl.pallas_call(
        products_kernel,
        out_shape=jax.ShapeDtypeStruct((16, 2, 8, 512), jnp.float32),
        in_specs=[
            pl.BlockSpec(memory_space=pltpu.SMEM),
            pl.BlockSpec(memory_space=pl.ANY),
            in_vmem,
            in_vmem,
        ],
        out_specs=in_vmem,
        scratch_shapes=[
            pltpu.VMEM((16, 112, 128), jnp.bfloat16),
            pltpu.SemaphoreType.DMA,
        ],
        compiler_params=pltpu.CompilerParams(vmem_limit_bytes=40 * 1024 * 1024),
        cost_estimate=pl.CostEstimate(
            flops=2 * 1792 * 256 * 512, bytes_accessed=4 * 1024 * 1024, transcendentals=0
        ),
    )(jnp.stack((mine, half)), tokens, got, cotangents)


def place_kernel(where_ref, source_ref, *refs):
    outs, done = refs[-4:-1], refs[-1]
    half = where_ref[0]
    copies = [
        pltpu.make_async_copy(source_ref.at[:, i], outs[i].at[half], done.at[i])
        for i in range(3)
    ]
    for copy in copies:
        copy.start()
    for copy in copies:
        copy.wait()


def place(half, source, outs=()):
    return pl.pallas_call(
        place_kernel,
        out_shape=[jax.ShapeDtypeStruct((2, 16, 8, 512), jnp.float32)] * 3,
        in_specs=[
            pl.BlockSpec(memory_space=pltpu.SMEM),
            pl.BlockSpec(memory_space=pltpu.VMEM),
        ]
        + [pl.BlockSpec(memory_space=pltpu.HBM)] * len(outs),
        out_specs=[pl.BlockSpec(memory_space=pltpu.HBM)] * 3,
        input_output_aliases={2 + i: i for i in range(len(outs))},
        scratch_shapes=[pltpu.SemaphoreType.DMA((3,))],
        compiler_params=pltpu.CompilerParams(vmem_limit_bytes=40 * 1024 * 1024),
        cost_estimate=pl.CostEstimate(
            flops=0, bytes_accessed=2 * 1024 * 1024, transcendentals=0
        ),
    )(half.reshape(1), source, *outs)


def on_device(activations, key_grads, partners, master_weight, first_moment, second_moment):
    mine = lax.axis_index("xh")
    other = 1 - mine
    core = lax.axis_index("c")
    column = lax.axis_index(("xl", "y"))

    def by_block(own, peer):
        return jnp.where(mine == 0, own, peer), jnp.where(mine == 0, peer, own)

    tokens = activations.reshape(16, 2, 112, 256)
    got = lax.ppermute(pick(tokens, other, 1), "xh", SWAP)

    first_row = 128 * core + 16 * column

    def eight(side, states):
        return jnp.stack(
            [
                lax.dynamic_slice_in_dim(
                    item, first_row + 8 * side, 8, axis=0, allow_negative_indices=False
                )
                for item in states
            ]
        )

    scaled = (key_grads.astype(jnp.float32) * KEY_SCALE).astype(jnp.float16)
    cotangents = lax.all_gather(scaled, "z", axis=0, tiled=True)
    cotangents = (cotangents.astype(jnp.float32) * (1.0 / KEY_SCALE)).astype(jnp.bfloat16)

    got = got.reshape(1792, 256)
    passed = lax.ppermute(products(mine, 1 - core, tokens, got, cotangents), "c", SWAP)
    partial = passed + products(mine, core, tokens, got, cotangents)
    pieces = exchange((partial * PARTIAL_SCALE).astype(jnp.float16), CHIPS)
    gradient = jnp.sum(pieces.astype(jnp.float32), axis=0) * (1.0 / PARTIAL_SCALE)

    states, partial = lax.optimization_barrier(
        ((master_weight, first_moment, second_moment), partial)
    )
    own_rows = eight(mine, states)
    peer_rows = lax.ppermute(eight(other, states), "xh", SWAP)

    old = jnp.stack(by_block(own_rows, peer_rows), axis=1)
    weight, moment_one, moment_two = adam_update(old[0], old[1], old[2], gradient)

    slices = jnp.stack((weight, moment_one, moment_two * SECOND_SCALE), axis=1)
    along = lax.all_gather(split_halves(slices).reshape(2, 48, 512), "z", axis=0)
    along = along.reshape(32, 2, 3, 8, 512)
    here = 2 * lax.axis_index("z")

    scales = jnp.where(jnp.arange(3) == 2, 1.0 / SECOND_SCALE, 1.0).reshape(3, 1, 1)

    def wanted(index):
        return join_halves(pick(along, pick(partners, index, 0), 0)) * scales

    placed = jnp.stack([wanted(here + i) for i in range(2)]).reshape(1, 2, 3, 8, 512)
    half = exchange(jnp.broadcast_to(placed, (8, 2, 3, 8, 512)).reshape(16, 3, 8, 512), CHIPS)
    sibling = lax.ppermute(half, "c", SWAP)
    outs = place(1 - core, sibling, place(core, half))
    return tuple(item.reshape(256, 512) for item in outs)


def solution(mesh):
    names = tuple(name for name, _ in PARTS)
    sizes = tuple(size for _, size in PARTS)
    fine = Mesh(mesh.devices.reshape(sizes), names)
    return jax.shard_map(
        on_device,
        mesh=fine,
        in_specs=(
            P(DP, FSDP),
            P(DP + FSDP, None),
            P(),
            P(FSDP, None),
            P(FSDP, None),
            P(FSDP, None),
        ),
        out_specs=(P(FSDP, None), P(FSDP, None), P(FSDP, None)),
        check_vma=False,
    )
```

```python
import jax
import jax.numpy as jnp
from jax import lax
from jax.experimental import pallas as pl
from jax.experimental.pallas import tpu as pltpu
from jax.sharding import Mesh
from jax.sharding import PartitionSpec as P

beta_first = 0.9
beta_second = 0.95
learn_rate = 0.01
weight_decay = 0.1
correct_first = 1.0 - 0.9**10
correct_second = 1.0 - 0.95**10

PARTS = (("xl", 2), ("y", 4), ("c", 2), ("z", 16), ("xh", 2))
DP = ("xl", "y", "c")
FSDP = ("z", "xh")
CHIPS = ("xl", "y", "xh")
PLANE = ("c", "xl", "y", "xh")
SWAP = [(0, 1), (1, 0)]
KEY_SCALE = 2.0**21
PARTIAL_SCALE = 2.0**7


def exchange(array, axes):
    return lax.all_to_all(array, axes, split_axis=0, concat_axis=0, tiled=True)


def pick(array, index, axis):
    return lax.dynamic_index_in_dim(
        array, index, axis=axis, keepdims=False, allow_negative_indices=False
    )


def adam_update(weight, first_moment, second_moment, gradient):
    new_first = beta_first * first_moment + (1.0 - beta_first) * gradient
    new_second = beta_second * second_moment + (1.0 - beta_second) * gradient * gradient
    step_size = new_first / correct_first / (jnp.sqrt(new_second / correct_second) + 1e-08)
    new_weight = weight - learn_rate * (step_size + weight_decay * weight)
    return (new_weight, new_first, new_second)


def products_kernel(mine_ref, tokens_ref, got_ref, cotangents_ref, out_ref, kept, arrived):
    mine = mine_ref[0]
    fetch = pltpu.make_async_copy(tokens_ref.at[:, mine], kept, arrived)
    fetch.start()

    def product(features):
        return lax.dot_general(
            features,
            cotangents_ref[...],
            (((0,), (0,)), ((), ())),
            preferred_element_type=jnp.float32,
        ).reshape(32, 8, 512)

    out_ref[:, 1 - mine] = product(got_ref[...])
    fetch.wait()
    out_ref[:, mine] = product(kept[...].reshape(1792, 256))


def products(mine, tokens, got, cotangents):
    in_vmem = pl.BlockSpec(memory_space=pltpu.VMEM)
    return pl.pallas_call(
        products_kernel,
        out_shape=jax.ShapeDtypeStruct((32, 2, 8, 512), jnp.float32),
        in_specs=[
            pl.BlockSpec(memory_space=pltpu.SMEM),
            pl.BlockSpec(memory_space=pl.ANY),
            in_vmem,
            in_vmem,
        ],
        out_specs=in_vmem,
        scratch_shapes=[
            pltpu.VMEM((16, 112, 256), jnp.bfloat16),
            pltpu.SemaphoreType.DMA,
        ],
        compiler_params=pltpu.CompilerParams(vmem_limit_bytes=40 * 1024 * 1024),
        cost_estimate=pl.CostEstimate(
            flops=2 * 2 * 1792 * 256 * 512, bytes_accessed=6 * 1024 * 1024, transcendentals=0
        ),
    )(mine.reshape(1), tokens, got, cotangents)


def assemble_kernel(core_ref, half_ref, sibling_ref, *refs):
    outs, done = refs[:3], refs[3]
    core = core_ref[0]
    copies = []
    for i in range(3):
        for j, (source, place) in enumerate(((half_ref, core), (sibling_ref, 1 - core))):
            copies.append(
                pltpu.make_async_copy(source.at[:, i], outs[i].at[place], done.at[2 * i + j])
            )
    for copy in copies:
        copy.start()
    for copy in copies:
        copy.wait()


def assemble(core, half, sibling):
    in_vmem = pl.BlockSpec(memory_space=pltpu.VMEM)
    outs = pl.pallas_call(
        assemble_kernel,
        out_shape=[jax.ShapeDtypeStruct((2, 16, 8, 512), jnp.float32)] * 3,
        in_specs=[pl.BlockSpec(memory_space=pltpu.SMEM), in_vmem, in_vmem],
        out_specs=[pl.BlockSpec(memory_space=pl.ANY)] * 3,
        scratch_shapes=[pltpu.SemaphoreType.DMA((6,))],
        compiler_params=pltpu.CompilerParams(vmem_limit_bytes=40 * 1024 * 1024),
    )(core.reshape(1), half, sibling)
    return tuple(item.reshape(256, 512) for item in outs)


def pick_kernel(partners_ref, spread_ref, out_ref):
    for j in range(32):
        out_ref[j] = spread_ref[partners_ref[j]]


def pick_blocks(spread, partners):
    return pl.pallas_call(
        pick_kernel,
        out_shape=jax.ShapeDtypeStruct(spread.shape, spread.dtype),
        in_specs=[
            pl.BlockSpec(memory_space=pltpu.SMEM),
            pl.BlockSpec(memory_space=pltpu.VMEM),
        ],
        out_specs=pl.BlockSpec(memory_space=pltpu.VMEM),
        compiler_params=pltpu.CompilerParams(vmem_limit_bytes=40 * 1024 * 1024),
    )(partners, spread)


def on_device(activations, key_grads, partners, master_weight, first_moment, second_moment):
    mine = lax.axis_index("xh")
    other = 1 - mine
    core = lax.axis_index("c")
    column = lax.axis_index(("xl", "y"))

    def by_block(own, peer):
        return jnp.where(mine == 0, own, peer), jnp.where(mine == 0, peer, own)

    tokens = activations.reshape(16, 2, 112, 256)
    got = lax.ppermute(pick(tokens, other, 1), "xh", SWAP)

    first_row = 128 * core + 16 * column

    def eight(side, states):
        return jnp.stack(
            [
                lax.dynamic_slice_in_dim(
                    item, first_row + 8 * side, 8, axis=0, allow_negative_indices=False
                )
                for item in states
            ]
        )

    scaled = (key_grads.astype(jnp.float32) * KEY_SCALE).astype(jnp.float16)
    cotangents = lax.all_gather(scaled, "z", axis=0, tiled=True)
    cotangents = (cotangents.astype(jnp.float32) * (1.0 / KEY_SCALE)).astype(jnp.bfloat16)

    partial = products(mine, tokens, got.reshape(1792, 256), cotangents)
    states, partial = lax.optimization_barrier(
        ((master_weight, first_moment, second_moment), partial)
    )
    pieces = exchange((partial * PARTIAL_SCALE).astype(jnp.float16), PLANE)
    gradient = jnp.sum(pieces.astype(jnp.float32), axis=0) * (1.0 / PARTIAL_SCALE)

    own_rows = eight(mine, states)
    peer_rows = lax.ppermute(eight(other, states), "xh", SWAP)
    old = jnp.stack(by_block(own_rows, peer_rows), axis=1)
    new = jnp.stack(adam_update(old[0], old[1], old[2], gradient))

    pieces = new.reshape(3, 2, 8, 2, 2, 128).transpose(2, 3, 1, 0, 4, 5).reshape(16, 2, 6, 128)
    pieces = jnp.pad(pieces, ((0, 0), (0, 0), (0, 2), (0, 0))).reshape(16, 16, 128)
    spread = exchange(pieces, "z").reshape(32, 8, 128)
    picked = pick_blocks(spread, partners).reshape(16, 16, 128)
    arrived = exchange(picked, "z").reshape(16, 2, 8, 128)[:, :, :6]
    placed = arrived.reshape(8, 2, 2, 3, 2, 128).transpose(2, 3, 0, 1, 4, 5)

    placed = placed.reshape(1, 2, 3, 8, 512)
    half = exchange(jnp.broadcast_to(placed, (8, 2, 3, 8, 512)).reshape(16, 3, 8, 512), CHIPS)
    sibling = lax.ppermute(half, "c", SWAP)
    return assemble(core, half, sibling)


def solution(mesh):
    names = tuple(name for name, _ in PARTS)
    sizes = tuple(size for _, size in PARTS)
    fine = Mesh(mesh.devices.reshape(sizes), names)
    return jax.shard_map(
        on_device,
        mesh=fine,
        in_specs=(
            P(DP, FSDP),
            P(DP + FSDP, None),
            P(),
            P(FSDP, None),
            P(FSDP, None),
            P(FSDP, None),
        ),
        out_specs=(P(FSDP, None), P(FSDP, None), P(FSDP, None)),
        check_vma=False,
    )
```

```python
import jax
import jax.numpy as jnp
from jax import lax
from jax.experimental import pallas as pl
from jax.experimental.pallas import tpu as pltpu
from jax.sharding import Mesh
from jax.sharding import PartitionSpec as P

beta_first = 0.9
beta_second = 0.95
learn_rate = 0.01
weight_decay = 0.1
correct_first = 1.0 - 0.9**10
correct_second = 1.0 - 0.95**10

PARTS = (("xl", 2), ("y", 4), ("c", 2), ("z", 16), ("xh", 2))
DP = ("xl", "y", "c")
FSDP = ("z", "xh")
CHIPS = ("xl", "y", "xh")
PLANE = ("c", "xl", "y", "xh")
SWAP = [(0, 1), (1, 0)]
KEY_SCALE = 2.0**21
REST_SCALE = 2.0**11
SECOND_SCALE = 2.0**-6
PARTIAL_SCALE = 2.0**7


def exchange(array, axes):
    return lax.all_to_all(array, axes, split_axis=0, concat_axis=0, tiled=True)


def pick(array, index, axis):
    return lax.dynamic_index_in_dim(
        array, index, axis=axis, keepdims=False, allow_negative_indices=False
    )


def split_halves(values):
    high = lax.reduce_precision(values, exponent_bits=5, mantissa_bits=10)
    rest = (values - high) * REST_SCALE
    return jnp.stack((high.astype(jnp.float16), rest.astype(jnp.float16)))


def join_halves(halves):
    wide = halves.astype(jnp.float32)
    return wide[0] + wide[1] * (1.0 / REST_SCALE)


def adam_update(weight, first_moment, second_moment, gradient):
    new_first = beta_first * first_moment + (1.0 - beta_first) * gradient
    new_second = beta_second * second_moment + (1.0 - beta_second) * gradient * gradient
    step_size = new_first / correct_first / (jnp.sqrt(new_second / correct_second) + 1e-08)
    new_weight = weight - learn_rate * (step_size + weight_decay * weight)
    return (new_weight, new_first, new_second)


def outgoing_kernel(other_ref, tokens_ref, out_ref, held, read, sent):
    other = other_ref[0]
    reads, sends = [], []
    for i in range(4):
        part = pl.ds(4 * i, 4)
        reads.append(
            pltpu.make_async_copy(tokens_ref.at[part, other], held.at[part], read.at[i])
        )
        sends.append(pltpu.make_async_copy(held.at[part], out_ref.at[part], sent.at[i]))
    for copy in reads:
        copy.start()
    for arriving, leaving in zip(reads, sends):
        arriving.wait()
        leaving.start()
    for copy in sends:
        copy.wait()


def outgoing(other, tokens):
    return pl.pallas_call(
        outgoing_kernel,
        out_shape=jax.ShapeDtypeStruct((16, 112, 256), jnp.bfloat16),
        in_specs=[
            pl.BlockSpec(memory_space=pltpu.SMEM),
            pl.BlockSpec(memory_space=pl.ANY),
        ],
        out_specs=pl.BlockSpec(memory_space=pl.ANY),
        scratch_shapes=[
            pltpu.VMEM((16, 112, 256), jnp.bfloat16),
            pltpu.SemaphoreType.DMA((4,)),
            pltpu.SemaphoreType.DMA((4,)),
        ],
        compiler_params=pltpu.CompilerParams(vmem_limit_bytes=56 * 1024 * 1024),
    )(other.reshape(1), tokens)


def products_kernel(mine_ref, tokens_ref, got_ref, cotangents_ref, out_ref, kept, arrived):
    mine = mine_ref[0]
    fetch = pltpu.make_async_copy(tokens_ref.at[:, mine], kept, arrived)
    fetch.start()

    def product(features):
        return lax.dot_general(
            features,
            cotangents_ref[...],
            (((0,), (0,)), ((), ())),
            preferred_element_type=jnp.float32,
        ).reshape(32, 8, 512)

    out_ref[:, 1 - mine] = product(got_ref[...])
    fetch.wait()
    out_ref[:, mine] = product(kept[...].reshape(1792, 256))


def products(mine, tokens, got, cotangents):
    in_vmem = pl.BlockSpec(memory_space=pltpu.VMEM)
    return pl.pallas_call(
        products_kernel,
        out_shape=jax.ShapeDtypeStruct((32, 2, 8, 512), jnp.float32),
        in_specs=[
            pl.BlockSpec(memory_space=pltpu.SMEM),
            pl.BlockSpec(memory_space=pl.ANY),
            in_vmem,
            in_vmem,
        ],
        out_specs=in_vmem,
        scratch_shapes=[
            pltpu.VMEM((16, 112, 256), jnp.bfloat16),
            pltpu.SemaphoreType.DMA,
        ],
        compiler_params=pltpu.CompilerParams(vmem_limit_bytes=40 * 1024 * 1024),
        cost_estimate=pl.CostEstimate(
            flops=2 * 2 * 1792 * 256 * 512, bytes_accessed=6 * 1024 * 1024, transcendentals=0
        ),
    )(mine.reshape(1), tokens, got, cotangents)


def assemble_kernel(core_ref, half_ref, sibling_ref, *refs):
    outs, done = refs[:3], refs[3]
    core = core_ref[0]
    copies = []
    for i in range(3):
        for j, (source, place) in enumerate(((half_ref, core), (sibling_ref, 1 - core))):
            copies.append(
                pltpu.make_async_copy(source.at[:, i], outs[i].at[place], done.at[2 * i + j])
            )
    for copy in copies:
        copy.start()
    for copy in copies:
        copy.wait()


def assemble(core, half, sibling):
    in_vmem = pl.BlockSpec(memory_space=pltpu.VMEM)
    outs = pl.pallas_call(
        assemble_kernel,
        out_shape=[jax.ShapeDtypeStruct((2, 16, 8, 512), jnp.float32)] * 3,
        in_specs=[pl.BlockSpec(memory_space=pltpu.SMEM), in_vmem, in_vmem],
        out_specs=[pl.BlockSpec(memory_space=pl.ANY)] * 3,
        scratch_shapes=[pltpu.SemaphoreType.DMA((6,))],
        compiler_params=pltpu.CompilerParams(vmem_limit_bytes=40 * 1024 * 1024),
    )(core.reshape(1), half, sibling)
    return tuple(item.reshape(256, 512) for item in outs)


def on_device(activations, key_grads, partners, master_weight, first_moment, second_moment):
    mine = lax.axis_index("xh")
    other = 1 - mine
    core = lax.axis_index("c")
    column = lax.axis_index(("xl", "y"))

    def by_block(own, peer):
        return jnp.where(mine == 0, own, peer), jnp.where(mine == 0, peer, own)

    tokens = activations.reshape(16, 2, 112, 256)
    got = lax.ppermute(outgoing(other, tokens), "xh", SWAP)

    first_row = 128 * core + 16 * column

    def eight(side, states):
        return jnp.stack(
            [
                lax.dynamic_slice_in_dim(
                    item, first_row + 8 * side, 8, axis=0, allow_negative_indices=False
                )
                for item in states
            ]
        )

    scaled = (key_grads.astype(jnp.float32) * KEY_SCALE).astype(jnp.float16)
    cotangents = lax.all_gather(scaled, "z", axis=0, tiled=True)
    cotangents = (cotangents.astype(jnp.float32) * (1.0 / KEY_SCALE)).astype(jnp.bfloat16)

    partial = products(mine, tokens, got.reshape(1792, 256), cotangents)
    states = (master_weight, first_moment, second_moment)
    pieces = exchange((partial * PARTIAL_SCALE).astype(jnp.float16), PLANE)
    gradient = jnp.sum(pieces.astype(jnp.float32), axis=0) * (1.0 / PARTIAL_SCALE)

    own_rows = eight(mine, states)
    peer_rows = lax.ppermute(eight(other, states), "xh", SWAP)
    old = jnp.stack(by_block(own_rows, peer_rows), axis=1)
    weight, moment_one, moment_two = adam_update(old[0], old[1], old[2], gradient)

    slices = jnp.stack((weight, moment_one, moment_two * SECOND_SCALE), axis=1)
    along = lax.all_gather(split_halves(slices), "z", axis=0, tiled=False)
    here = 2 * lax.axis_index("z")

    scales = jnp.array([1.0, 1.0, 1.0 / SECOND_SCALE], jnp.float32).reshape(3, 1, 1)

    def wanted(index):
        place = pick(partners, index, 0)
        return join_halves(pick(pick(along, place >> 1, 0), place & 1, 1)) * scales

    placed = jnp.stack([wanted(here + i) for i in range(2)]).reshape(1, 2, 3, 8, 512)
    half = exchange(jnp.broadcast_to(placed, (8, 2, 3, 8, 512)).reshape(16, 3, 8, 512), CHIPS)
    sibling = lax.ppermute(half, "c", SWAP)
    return assemble(core, half, sibling)


def solution(mesh):
    names = tuple(name for name, _ in PARTS)
    sizes = tuple(size for _, size in PARTS)
    fine = Mesh(mesh.devices.reshape(sizes), names)
    return jax.shard_map(
        on_device,
        mesh=fine,
        in_specs=(
            P(DP, FSDP),
            P(DP + FSDP, None),
            P(),
            P(FSDP, None),
            P(FSDP, None),
            P(FSDP, None),
        ),
        out_specs=(P(FSDP, None), P(FSDP, None), P(FSDP, None)),
        check_vma=False,
    )
```

```python
import jax
import jax.numpy as jnp
from jax import lax
from jax.experimental import pallas as pl
from jax.experimental.pallas import tpu as pltpu
from jax.sharding import Mesh
from jax.sharding import PartitionSpec as P

beta_first = 0.9
beta_second = 0.95
learn_rate = 0.01
weight_decay = 0.1
correct_first = 1.0 - 0.9**10
correct_second = 1.0 - 0.95**10

PARTS = (("xl", 2), ("y", 4), ("c", 2), ("zb", 4), ("za", 4), ("xh", 2))
DP = ("xl", "y", "c")
FSDP = ("zb", "za", "xh")
Z = ("zb", "za")
CHIPS = ("xl", "y", "xh")
PLANE = ("c", "xl", "y", "xh")
SWAP = [(0, 1), (1, 0)]
KEY_SCALE = 2.0**21
PARTIAL_SCALE = 2.0**7


def exchange(array, axes):
    return lax.all_to_all(array, axes, split_axis=0, concat_axis=0, tiled=True)


def pick(array, index, axis):
    return lax.dynamic_index_in_dim(
        array, index, axis=axis, keepdims=False, allow_negative_indices=False
    )


def adam_update(weight, first_moment, second_moment, gradient):
    new_first = beta_first * first_moment + (1.0 - beta_first) * gradient
    new_second = beta_second * second_moment + (1.0 - beta_second) * gradient * gradient
    step_size = new_first / correct_first / (jnp.sqrt(new_second / correct_second) + 1e-08)
    new_weight = weight - learn_rate * (step_size + weight_decay * weight)
    return (new_weight, new_first, new_second)


def products_kernel(mine_ref, tokens_ref, got_ref, cotangents_ref, out_ref, kept, arrived):
    mine = mine_ref[0]
    fetch = pltpu.make_async_copy(tokens_ref.at[:, mine], kept, arrived)
    fetch.start()

    def product(features):
        return lax.dot_general(
            features,
            cotangents_ref[...],
            (((0,), (0,)), ((), ())),
            preferred_element_type=jnp.float32,
        ).reshape(32, 8, 512)

    out_ref[:, 1 - mine] = product(got_ref[...])
    fetch.wait()
    out_ref[:, mine] = product(kept[...].reshape(1792, 256))


def products(mine, tokens, got, cotangents):
    in_vmem = pl.BlockSpec(memory_space=pltpu.VMEM)
    return pl.pallas_call(
        products_kernel,
        out_shape=jax.ShapeDtypeStruct((32, 2, 8, 512), jnp.float32),
        in_specs=[
            pl.BlockSpec(memory_space=pltpu.SMEM),
            pl.BlockSpec(memory_space=pl.ANY),
            in_vmem,
            in_vmem,
        ],
        out_specs=in_vmem,
        scratch_shapes=[
            pltpu.VMEM((16, 112, 256), jnp.bfloat16),
            pltpu.SemaphoreType.DMA,
        ],
        compiler_params=pltpu.CompilerParams(vmem_limit_bytes=40 * 1024 * 1024),
        cost_estimate=pl.CostEstimate(
            flops=2 * 2 * 1792 * 256 * 512, bytes_accessed=6 * 1024 * 1024, transcendentals=0
        ),
    )(mine.reshape(1), tokens, got, cotangents)


def assemble_kernel(core_ref, half_ref, sibling_ref, *refs):
    outs, done = refs[:3], refs[3]
    core = core_ref[0]
    copies = []
    for i in range(3):
        for j, (source, place) in enumerate(((half_ref, core), (sibling_ref, 1 - core))):
            copies.append(
                pltpu.make_async_copy(source.at[:, i], outs[i].at[place], done.at[2 * i + j])
            )
    for copy in copies:
        copy.start()
    for copy in copies:
        copy.wait()


def assemble(core, half, sibling):
    in_vmem = pl.BlockSpec(memory_space=pltpu.VMEM)
    outs = pl.pallas_call(
        assemble_kernel,
        out_shape=[jax.ShapeDtypeStruct((2, 16, 8, 512), jnp.float32)] * 3,
        in_specs=[pl.BlockSpec(memory_space=pltpu.SMEM), in_vmem, in_vmem],
        out_specs=[pl.BlockSpec(memory_space=pl.ANY)] * 3,
        scratch_shapes=[pltpu.SemaphoreType.DMA((6,))],
        compiler_params=pltpu.CompilerParams(vmem_limit_bytes=40 * 1024 * 1024),
    )(core.reshape(1), half, sibling)
    return tuple(item.reshape(256, 512) for item in outs)


def offer_kernel(group_ref, partners_ref, held_ref, out_ref):
    for i in range(8):
        partner = partners_ref[8 * group_ref[0] + i]
        out_ref[i] = held_ref[2 * (partner >> 3) + (partner & 1)]


def take_kernel(place_ref, partners_ref, offered_ref, out_ref):
    for i in range(2):
        partner = partners_ref[2 * place_ref[0] + i]
        block = offered_ref[(partner >> 1) & 3, i]
        for k in range(8):
            out_ref[k, i] = block


def pick_blocks(kernel, position, partners, source, shape):
    in_smem = pl.BlockSpec(memory_space=pltpu.SMEM)
    in_vmem = pl.BlockSpec(memory_space=pltpu.VMEM)
    return pl.pallas_call(
        kernel,
        out_shape=jax.ShapeDtypeStruct(shape, source.dtype),
        in_specs=[in_smem, in_smem, in_vmem],
        out_specs=in_vmem,
        compiler_params=pltpu.CompilerParams(vmem_limit_bytes=40 * 1024 * 1024),
    )(position.reshape(1), partners, source)


def on_device(activations, key_grads, partners, master_weight, first_moment, second_moment):
    mine = lax.axis_index("xh")
    other = 1 - mine
    core = lax.axis_index("c")
    column = lax.axis_index(("xl", "y"))

    def by_block(own, peer):
        return jnp.where(mine == 0, own, peer), jnp.where(mine == 0, peer, own)

    tokens = activations.reshape(16, 2, 112, 256)
    got = lax.ppermute(pick(tokens, other, 1), "xh", SWAP)

    first_row = 128 * core + 16 * column

    def eight(side, states):
        return jnp.stack(
            [
                lax.dynamic_slice_in_dim(
                    item, first_row + 8 * side, 8, axis=0, allow_negative_indices=False
                )
                for item in states
            ]
        )

    scaled = (key_grads.astype(jnp.float32) * KEY_SCALE).astype(jnp.float16)
    cotangents = lax.all_gather(scaled, Z, axis=0, tiled=True)
    cotangents = (cotangents.astype(jnp.float32) * (1.0 / KEY_SCALE)).astype(jnp.bfloat16)

    partial = products(mine, tokens, got.reshape(1792, 256), cotangents)
    states = (master_weight, first_moment, second_moment)
    pieces = exchange((partial * PARTIAL_SCALE).astype(jnp.float16), PLANE)
    gradient = jnp.sum(pieces.astype(jnp.float32), axis=0) * (1.0 / PARTIAL_SCALE)

    own_rows = eight(mine, states)
    peer_rows = lax.ppermute(eight(other, states), "xh", SWAP)
    old = jnp.stack(by_block(own_rows, peer_rows), axis=1)
    results = jnp.stack(adam_update(old[0], old[1], old[2], gradient), axis=1)

    held = lax.all_gather(results.reshape(2, 24, 512), "zb", axis=0, tiled=True)
    offers = pick_blocks(offer_kernel, lax.axis_index("zb"), partners, held, (8, 24, 512))
    offered = exchange(offers.reshape(4, 2, 24, 512), "za")
    placed = pick_blocks(take_kernel, lax.axis_index(Z), partners, offered, (8, 2, 24, 512))

    half = exchange(placed.reshape(16, 3, 8, 512), CHIPS)
    sibling = lax.ppermute(half, "c", SWAP)
    return assemble(core, half, sibling)


def solution(mesh):
    names = tuple(name for name, _ in PARTS)
    sizes = tuple(size for _, size in PARTS)
    fine = Mesh(mesh.devices.reshape(sizes), names)
    return jax.shard_map(
        on_device,
        mesh=fine,
        in_specs=(
            P(DP, FSDP),
            P(DP + FSDP, None),
            P(),
            P(FSDP, None),
            P(FSDP, None),
            P(FSDP, None),
        ),
        out_specs=(P(FSDP, None), P(FSDP, None), P(FSDP, None)),
        check_vma=False,
    )
```

```python
import jax
import jax.numpy as jnp
from jax import lax
from jax.experimental import pallas as pl
from jax.experimental.pallas import tpu as pltpu
from jax.sharding import Mesh
from jax.sharding import PartitionSpec as P

beta_first = 0.9
beta_second = 0.95
learn_rate = 0.01
weight_decay = 0.1
correct_first = 1.0 - 0.9**10
correct_second = 1.0 - 0.95**10

PARTS = (("xl", 2), ("y", 4), ("c", 2), ("z", 16), ("xh", 2))
DP = ("xl", "y", "c")
FSDP = ("z", "xh")
CHIPS = ("xl", "y", "xh")
PLANE = ("c", "xl", "y", "xh")
SWAP = [(0, 1), (1, 0)]
KEY_SCALE = 2.0**21
REST_SCALE = 2.0**11
SECOND_SCALE = 2.0**-6
PARTIAL_SCALE = 2.0**7


def exchange(array, axes):
    return lax.all_to_all(array, axes, split_axis=0, concat_axis=0, tiled=True)


def pick(array, index, axis):
    return lax.dynamic_index_in_dim(
        array, index, axis=axis, keepdims=False, allow_negative_indices=False
    )


def split_halves(values):
    high = lax.reduce_precision(values, exponent_bits=5, mantissa_bits=10)
    rest = (values - high) * REST_SCALE
    return jnp.stack((high.astype(jnp.float16), rest.astype(jnp.float16)))


def join_halves(halves):
    wide = halves.astype(jnp.float32)
    return wide[0] + wide[1] * (1.0 / REST_SCALE)


def adam_update(weight, first_moment, second_moment, gradient):
    new_first = beta_first * first_moment + (1.0 - beta_first) * gradient
    new_second = beta_second * second_moment + (1.0 - beta_second) * gradient * gradient
    step_size = new_first / correct_first / (jnp.sqrt(new_second / correct_second) + 1e-08)
    new_weight = weight - learn_rate * (step_size + weight_decay * weight)
    return (new_weight, new_first, new_second)


def products_kernel(mine_ref, tokens_ref, got_ref, cotangents_ref, out_ref, kept, arrived):
    mine = mine_ref[0]
    fetch = pltpu.make_async_copy(tokens_ref.at[:, mine], kept, arrived)
    fetch.start()

    def product(features):
        return lax.dot_general(
            features,
            cotangents_ref[...],
            (((0,), (0,)), ((), ())),
            preferred_element_type=jnp.float32,
        ).reshape(32, 8, 512)

    out_ref[:, 1 - mine] = product(got_ref[...])
    fetch.wait()
    out_ref[:, mine] = product(kept[...].reshape(1792, 256))


def products(mine, tokens, got, cotangents):
    in_vmem = pl.BlockSpec(memory_space=pltpu.VMEM)
    return pl.pallas_call(
        products_kernel,
        out_shape=jax.ShapeDtypeStruct((32, 2, 8, 512), jnp.float32),
        in_specs=[
            pl.BlockSpec(memory_space=pltpu.SMEM),
            pl.BlockSpec(memory_space=pl.ANY),
            in_vmem,
            in_vmem,
        ],
        out_specs=in_vmem,
        scratch_shapes=[
            pltpu.VMEM((16, 112, 256), jnp.bfloat16),
            pltpu.SemaphoreType.DMA,
        ],
        compiler_params=pltpu.CompilerParams(vmem_limit_bytes=40 * 1024 * 1024),
        cost_estimate=pl.CostEstimate(
            flops=2 * 2 * 1792 * 256 * 512, bytes_accessed=6 * 1024 * 1024, transcendentals=0
        ),
    )(mine.reshape(1), tokens, got, cotangents)


def assemble_kernel(core_ref, half_ref, sibling_ref, *refs):
    outs, done = refs[:3], refs[3]
    core = core_ref[0]
    copies = []
    for i in range(3):
        for j, (source, place) in enumerate(((half_ref, core), (sibling_ref, 1 - core))):
            copies.append(
                pltpu.make_async_copy(source.at[:, i], outs[i].at[place], done.at[2 * i + j])
            )
    for copy in copies:
        copy.start()
    for copy in copies:
        copy.wait()


def assemble(core, half, sibling):
    in_vmem = pl.BlockSpec(memory_space=pltpu.VMEM)
    outs = pl.pallas_call(
        assemble_kernel,
        out_shape=[jax.ShapeDtypeStruct((2, 16, 8, 512), jnp.float32)] * 3,
        in_specs=[pl.BlockSpec(memory_space=pltpu.SMEM), in_vmem, in_vmem],
        out_specs=[pl.BlockSpec(memory_space=pl.ANY)] * 3,
        scratch_shapes=[pltpu.SemaphoreType.DMA((6,))],
        compiler_params=pltpu.CompilerParams(vmem_limit_bytes=40 * 1024 * 1024),
    )(core.reshape(1), half, sibling)
    return tuple(item.reshape(256, 512) for item in outs)


def on_device(activations, key_grads, partners, master_weight, first_moment, second_moment):
    mine = lax.axis_index("xh")
    other = 1 - mine
    core = lax.axis_index("c")
    column = lax.axis_index(("xl", "y"))

    def by_block(own, peer):
        return jnp.where(mine == 0, own, peer), jnp.where(mine == 0, peer, own)

    tokens = activations.reshape(16, 2, 112, 256)
    got = lax.ppermute(pick(tokens, other, 1), "xh", SWAP)

    first_row = 128 * core + 16 * column

    def eight(side):
        return jnp.stack(
            [
                lax.dynamic_slice_in_dim(
                    item, first_row + 8 * side, 8, axis=0, allow_negative_indices=False
                )
                for item in (master_weight, first_moment, second_moment)
            ]
        )

    scaled = (key_grads.astype(jnp.float32) * KEY_SCALE).astype(jnp.float16)
    cotangents = lax.all_gather(scaled, "z", axis=0, tiled=True)
    got, cotangents = lax.optimization_barrier((got, cotangents))
    own_rows = eight(mine)
    peer_rows = lax.ppermute(eight(other), "xh", SWAP)
    cotangents = (cotangents.astype(jnp.float32) * (1.0 / KEY_SCALE)).astype(jnp.bfloat16)

    partial = products(mine, tokens, got.reshape(1792, 256), cotangents)
    pieces = exchange((partial * PARTIAL_SCALE).astype(jnp.float16), PLANE)
    gradient = jnp.sum(pieces.astype(jnp.float32), axis=0) * (1.0 / PARTIAL_SCALE)

    old = jnp.stack(by_block(own_rows, peer_rows), axis=1)
    weight, moment_one, moment_two = adam_update(old[0], old[1], old[2], gradient)

    slices = jnp.stack((weight, moment_one, moment_two * SECOND_SCALE), axis=1)
    along = lax.all_gather(split_halves(slices), "z", axis=0, tiled=False)
    here = 2 * lax.axis_index("z")

    scales = jnp.array([1.0, 1.0, 1.0 / SECOND_SCALE], jnp.float32).reshape(3, 1, 1)

    def wanted(index):
        place = pick(partners, index, 0)
        return join_halves(pick(pick(along, place >> 1, 0), place & 1, 1)) * scales

    placed = jnp.stack([wanted(here + i) for i in range(2)]).reshape(1, 2, 3, 8, 512)
    half = exchange(jnp.broadcast_to(placed, (8, 2, 3, 8, 512)).reshape(16, 3, 8, 512), CHIPS)
    sibling = lax.ppermute(half, "c", SWAP)
    return assemble(core, half, sibling)


def solution(mesh):
    names = tuple(name for name, _ in PARTS)
    sizes = tuple(size for _, size in PARTS)
    fine = Mesh(mesh.devices.reshape(sizes), names)
    return jax.shard_map(
        on_device,
        mesh=fine,
        in_specs=(
            P(DP, FSDP),
            P(DP + FSDP, None),
            P(),
            P(FSDP, None),
            P(FSDP, None),
            P(FSDP, None),
        ),
        out_specs=(P(FSDP, None), P(FSDP, None), P(FSDP, None)),
        check_vma=False,
    )
```

```python
import jax
import jax.numpy as jnp
from jax import lax
from jax.experimental import pallas as pl
from jax.experimental.pallas import tpu as pltpu
from jax.sharding import Mesh
from jax.sharding import PartitionSpec as P

beta_first = 0.9
beta_second = 0.95
learn_rate = 0.01
weight_decay = 0.1
correct_first = 1.0 - 0.9**10
correct_second = 1.0 - 0.95**10

PARTS = (("xl", 2), ("y", 4), ("c", 2), ("z", 16), ("xh", 2))
DP = ("xl", "y", "c")
FSDP = ("z", "xh")
CHIPS = ("xl", "y", "xh")
PLANE = ("c", "xl", "y", "xh")
SWAP = [(0, 1), (1, 0)]
KEY_SCALE = 2.0**21
REST_SCALE = 2.0**11
FIRST_SCALE = 2.0**6
SECOND_SCALE = 2.0**-6
PARTIAL_SCALE = 2.0**7


def exchange(array, axes):
    return lax.all_to_all(array, axes, split_axis=0, concat_axis=0, tiled=True)


def pick(array, index, axis):
    return lax.dynamic_index_in_dim(
        array, index, axis=axis, keepdims=False, allow_negative_indices=False
    )


def pack(weight, moment_one, moment_two):
    high = lax.reduce_precision(weight, exponent_bits=5, mantissa_bits=10)
    rest = (weight - high) * REST_SCALE
    return jnp.stack((high, rest, moment_one * FIRST_SCALE, moment_two * SECOND_SCALE)).astype(
        jnp.float16
    )


def unpack(packed):
    wide = packed.astype(jnp.float32)
    return jnp.stack(
        (
            wide[0] + wide[1] * (1.0 / REST_SCALE),
            wide[2] * (1.0 / FIRST_SCALE),
            wide[3] * (1.0 / SECOND_SCALE),
        )
    )


def adam_update(weight, first_moment, second_moment, gradient):
    new_first = beta_first * first_moment + (1.0 - beta_first) * gradient
    new_second = beta_second * second_moment + (1.0 - beta_second) * gradient * gradient
    step_size = new_first / correct_first / (jnp.sqrt(new_second / correct_second) + 1e-08)
    new_weight = weight - learn_rate * (step_size + weight_decay * weight)
    return (new_weight, new_first, new_second)


def products_kernel(mine_ref, tokens_ref, got_ref, cotangents_ref, out_ref, kept, arrived):
    mine = mine_ref[0]
    fetch = pltpu.make_async_copy(tokens_ref.at[:, mine], kept, arrived)
    fetch.start()

    def product(features):
        return lax.dot_general(
            features,
            cotangents_ref[...],
            (((0,), (0,)), ((), ())),
            preferred_element_type=jnp.float32,
        ).reshape(32, 8, 512)

    out_ref[:, 1 - mine] = product(got_ref[...])
    fetch.wait()
    out_ref[:, mine] = product(kept[...].reshape(1792, 256))


def products(mine, tokens, got, cotangents):
    in_vmem = pl.BlockSpec(memory_space=pltpu.VMEM)
    return pl.pallas_call(
        products_kernel,
        out_shape=jax.ShapeDtypeStruct((32, 2, 8, 512), jnp.float32),
        in_specs=[
            pl.BlockSpec(memory_space=pltpu.SMEM),
            pl.BlockSpec(memory_space=pl.ANY),
            in_vmem,
            in_vmem,
        ],
        out_specs=in_vmem,
        scratch_shapes=[
            pltpu.VMEM((16, 112, 256), jnp.bfloat16),
            pltpu.SemaphoreType.DMA,
        ],
        compiler_params=pltpu.CompilerParams(vmem_limit_bytes=40 * 1024 * 1024),
        cost_estimate=pl.CostEstimate(
            flops=2 * 2 * 1792 * 256 * 512, bytes_accessed=6 * 1024 * 1024, transcendentals=0
        ),
    )(mine.reshape(1), tokens, got, cotangents)


def assemble_kernel(core_ref, half_ref, sibling_ref, *refs):
    outs, done = refs[:3], refs[3]
    core = core_ref[0]
    copies = []
    for i in range(3):
        for j, (source, place) in enumerate(((half_ref, core), (sibling_ref, 1 - core))):
            copies.append(
                pltpu.make_async_copy(source.at[:, i], outs[i].at[place], done.at[2 * i + j])
            )
    for copy in copies:
        copy.start()
    for copy in copies:
        copy.wait()


def assemble(core, half, sibling):
    in_vmem = pl.BlockSpec(memory_space=pltpu.VMEM)
    outs = pl.pallas_call(
        assemble_kernel,
        out_shape=[jax.ShapeDtypeStruct((2, 16, 8, 512), jnp.float32)] * 3,
        in_specs=[pl.BlockSpec(memory_space=pltpu.SMEM), in_vmem, in_vmem],
        out_specs=[pl.BlockSpec(memory_space=pl.ANY)] * 3,
        scratch_shapes=[pltpu.SemaphoreType.DMA((6,))],
        compiler_params=pltpu.CompilerParams(vmem_limit_bytes=40 * 1024 * 1024),
    )(core.reshape(1), half, sibling)
    return tuple(item.reshape(256, 512) for item in outs)


def on_device(activations, key_grads, partners, master_weight, first_moment, second_moment):
    mine = lax.axis_index("xh")
    other = 1 - mine
    core = lax.axis_index("c")
    column = lax.axis_index(("xl", "y"))

    def by_block(own, peer):
        return jnp.where(mine == 0, own, peer), jnp.where(mine == 0, peer, own)

    tokens = activations.reshape(16, 2, 112, 256)
    got = lax.ppermute(pick(tokens, other, 1), "xh", SWAP)

    first_row = 128 * core + 16 * column

    def eight(side):
        return jnp.stack(
            [
                lax.dynamic_slice_in_dim(
                    item, first_row + 8 * side, 8, axis=0, allow_negative_indices=False
                )
                for item in (master_weight, first_moment, second_moment)
            ]
        )

    scaled = (key_grads.astype(jnp.float32) * KEY_SCALE).astype(jnp.float16)
    cotangents = lax.all_gather(scaled, "z", axis=0, tiled=True)
    got, cotangents = lax.optimization_barrier((got, cotangents))
    own_rows = eight(mine)
    peer_rows = lax.ppermute(eight(other), "xh", SWAP)
    cotangents = (cotangents.astype(jnp.float32) * (1.0 / KEY_SCALE)).astype(jnp.bfloat16)

    partial = products(mine, tokens, got.reshape(1792, 256), cotangents)
    pieces = exchange((partial * PARTIAL_SCALE).astype(jnp.float16), PLANE)
    gradient = jnp.sum(pieces.astype(jnp.float32), axis=0) * (1.0 / PARTIAL_SCALE)

    old = jnp.stack(by_block(own_rows, peer_rows), axis=1)
    results = adam_update(old[0], old[1], old[2], gradient)

    along = lax.all_gather(pack(*results), "z", axis=0, tiled=False)
    here = 2 * lax.axis_index("z")

    def wanted(index):
        place = pick(partners, index, 0)
        return unpack(pick(pick(along, place >> 1, 0), place & 1, 1))

    placed = jnp.stack([wanted(here + i) for i in range(2)]).reshape(1, 2, 3, 8, 512)
    half = exchange(jnp.broadcast_to(placed, (8, 2, 3, 8, 512)).reshape(16, 3, 8, 512), CHIPS)
    sibling = lax.ppermute(half, "c", SWAP)
    return assemble(core, half, sibling)


def solution(mesh):
    names = tuple(name for name, _ in PARTS)
    sizes = tuple(size for _, size in PARTS)
    fine = Mesh(mesh.devices.reshape(sizes), names)
    return jax.shard_map(
        on_device,
        mesh=fine,
        in_specs=(
            P(DP, FSDP),
            P(DP + FSDP, None),
            P(),
            P(FSDP, None),
            P(FSDP, None),
            P(FSDP, None),
        ),
        out_specs=(P(FSDP, None), P(FSDP, None), P(FSDP, None)),
        check_vma=False,
    )
```

```python
import jax
import jax.numpy as jnp
from jax import lax
from jax.experimental import pallas as pl
from jax.experimental.pallas import tpu as pltpu
from jax.sharding import Mesh
from jax.sharding import PartitionSpec as P

beta_first = 0.9
beta_second = 0.95
learn_rate = 0.01
weight_decay = 0.1
correct_first = 1.0 - 0.9**10
correct_second = 1.0 - 0.95**10

PARTS = (("xl", 2), ("y", 4), ("c", 2), ("z", 16), ("xh", 2))
DP = ("xl", "y", "c")
FSDP = ("z", "xh")
CHIPS = ("xl", "y", "xh")
PLANE = ("c", "xl", "y", "xh")
SWAP = [(0, 1), (1, 0)]
KEY_SCALE = 2.0**21
REST_SCALE = 2.0**11
FIRST_SCALE = 2.0**6
SECOND_SCALE = 2.0**-6
PARTIAL_SCALE = 2.0**7


def exchange(array, axes):
    return lax.all_to_all(array, axes, split_axis=0, concat_axis=0, tiled=True)


def pick(array, index, axis):
    return lax.dynamic_index_in_dim(
        array, index, axis=axis, keepdims=False, allow_negative_indices=False
    )


def pack(weight, moment_one, moment_two):
    high = lax.reduce_precision(weight, exponent_bits=5, mantissa_bits=10)
    rest = (weight - high) * REST_SCALE
    return jnp.stack((high, rest, moment_one * FIRST_SCALE, moment_two * SECOND_SCALE)).astype(
        jnp.float16
    )


def unpack(packed):
    wide = packed.astype(jnp.float32)
    return jnp.stack(
        (
            wide[:, 0] + wide[:, 1] * (1.0 / REST_SCALE),
            wide[:, 2] * (1.0 / FIRST_SCALE),
            wide[:, 3] * (1.0 / SECOND_SCALE),
        ),
        axis=1,
    )


def adam_update(weight, first_moment, second_moment, gradient):
    new_first = beta_first * first_moment + (1.0 - beta_first) * gradient
    new_second = beta_second * second_moment + (1.0 - beta_second) * gradient * gradient
    step_size = new_first / correct_first / (jnp.sqrt(new_second / correct_second) + 1e-08)
    new_weight = weight - learn_rate * (step_size + weight_decay * weight)
    return (new_weight, new_first, new_second)


def products_kernel(mine_ref, tokens_ref, got_ref, cotangents_ref, out_ref, kept, arrived):
    mine = mine_ref[0]
    fetch = pltpu.make_async_copy(tokens_ref.at[:, mine], kept, arrived)
    fetch.start()

    def product(features):
        return lax.dot_general(
            features,
            cotangents_ref[...],
            (((0,), (0,)), ((), ())),
            preferred_element_type=jnp.float32,
        ).reshape(32, 8, 512)

    out_ref[:, 1 - mine] = product(got_ref[...])
    fetch.wait()
    out_ref[:, mine] = product(kept[...].reshape(1792, 256))


def products(mine, tokens, got, cotangents):
    in_vmem = pl.BlockSpec(memory_space=pltpu.VMEM)
    return pl.pallas_call(
        products_kernel,
        out_shape=jax.ShapeDtypeStruct((32, 2, 8, 512), jnp.float32),
        in_specs=[
            pl.BlockSpec(memory_space=pltpu.SMEM),
            pl.BlockSpec(memory_space=pl.ANY),
            in_vmem,
            in_vmem,
        ],
        out_specs=in_vmem,
        scratch_shapes=[
            pltpu.VMEM((16, 112, 256), jnp.bfloat16),
            pltpu.SemaphoreType.DMA,
        ],
        compiler_params=pltpu.CompilerParams(vmem_limit_bytes=40 * 1024 * 1024),
        cost_estimate=pl.CostEstimate(
            flops=2 * 2 * 1792 * 256 * 512, bytes_accessed=6 * 1024 * 1024, transcendentals=0
        ),
    )(mine.reshape(1), tokens, got, cotangents)


def assemble_kernel(core_ref, half_ref, sibling_ref, *refs):
    outs, done = refs[:3], refs[3]
    core = core_ref[0]
    copies = []
    for i in range(3):
        for j, (source, place) in enumerate(((half_ref, core), (sibling_ref, 1 - core))):
            copies.append(
                pltpu.make_async_copy(source.at[:, i], outs[i].at[place], done.at[2 * i + j])
            )
    for copy in copies:
        copy.start()
    for copy in copies:
        copy.wait()


def assemble(core, half, sibling):
    in_vmem = pl.BlockSpec(memory_space=pltpu.VMEM)
    outs = pl.pallas_call(
        assemble_kernel,
        out_shape=[jax.ShapeDtypeStruct((2, 16, 8, 512), jnp.float32)] * 3,
        in_specs=[pl.BlockSpec(memory_space=pltpu.SMEM), in_vmem, in_vmem],
        out_specs=[pl.BlockSpec(memory_space=pl.ANY)] * 3,
        scratch_shapes=[pltpu.SemaphoreType.DMA((6,))],
        compiler_params=pltpu.CompilerParams(vmem_limit_bytes=40 * 1024 * 1024),
    )(core.reshape(1), half, sibling)
    return tuple(item.reshape(256, 512) for item in outs)


def on_device(activations, key_grads, partners, master_weight, first_moment, second_moment):
    mine = lax.axis_index("xh")
    other = 1 - mine
    core = lax.axis_index("c")
    column = lax.axis_index(("xl", "y"))

    def by_block(own, peer):
        return jnp.where(mine == 0, own, peer), jnp.where(mine == 0, peer, own)

    tokens = activations.reshape(16, 2, 112, 256)
    got = lax.ppermute(pick(tokens, other, 1), "xh", SWAP)

    first_row = 128 * core + 16 * column

    def eight(side):
        return jnp.stack(
            [
                lax.dynamic_slice_in_dim(
                    item, first_row + 8 * side, 8, axis=0, allow_negative_indices=False
                )
                for item in (master_weight, first_moment, second_moment)
            ]
        )

    scaled = (key_grads.astype(jnp.float32) * KEY_SCALE).astype(jnp.float16)
    cotangents = lax.all_gather(scaled, "z", axis=0, tiled=True)
    got, cotangents = lax.optimization_barrier((got, cotangents))
    own_rows = eight(mine)
    peer_rows = lax.ppermute(eight(other), "xh", SWAP)
    cotangents = (cotangents.astype(jnp.float32) * (1.0 / KEY_SCALE)).astype(jnp.bfloat16)

    partial = products(mine, tokens, got.reshape(1792, 256), cotangents)
    pieces = exchange((partial * PARTIAL_SCALE).astype(jnp.float16), PLANE)
    gradient = jnp.sum(pieces.astype(jnp.float32), axis=0) * (1.0 / PARTIAL_SCALE)

    old = jnp.stack(by_block(own_rows, peer_rows), axis=1)
    results = adam_update(old[0], old[1], old[2], gradient)

    along = lax.all_gather(pack(*results), "z", axis=0, tiled=False)
    here = 2 * lax.axis_index("z")

    def wanted(index):
        place = pick(partners, index, 0)
        return pick(pick(along, place >> 1, 0), place & 1, 1)

    placed = jnp.stack([wanted(here + i) for i in range(2)]).reshape(1, 2, 4, 8, 512)
    shared = jnp.broadcast_to(placed, (8, 2, 4, 8, 512)).reshape(16, 4, 8, 512)
    half = unpack(exchange(shared, CHIPS))
    sibling = lax.ppermute(half, "c", SWAP)
    return assemble(core, half, sibling)


def solution(mesh):
    names = tuple(name for name, _ in PARTS)
    sizes = tuple(size for _, size in PARTS)
    fine = Mesh(mesh.devices.reshape(sizes), names)
    return jax.shard_map(
        on_device,
        mesh=fine,
        in_specs=(
            P(DP, FSDP),
            P(DP + FSDP, None),
            P(),
            P(FSDP, None),
            P(FSDP, None),
            P(FSDP, None),
        ),
        out_specs=(P(FSDP, None), P(FSDP, None), P(FSDP, None)),
        check_vma=False,
    )
```

```python
import jax
import jax.numpy as jnp
from jax import lax
from jax.experimental import pallas as pl
from jax.experimental.pallas import tpu as pltpu
from jax.sharding import Mesh
from jax.sharding import PartitionSpec as P

beta_first = 0.9
beta_second = 0.95
learn_rate = 0.01
weight_decay = 0.1
correct_first = 1.0 - 0.9**10
correct_second = 1.0 - 0.95**10

PARTS = (("xl", 2), ("y", 4), ("c", 2), ("z", 16), ("xh", 2))
DP = ("xl", "y", "c")
FSDP = ("z", "xh")
CHIPS = ("xl", "y", "xh")
PLANE = ("c", "xl", "y", "xh")
SWAP = [(0, 1), (1, 0)]
KEY_SCALE = 2.0**21
REST_SCALE = 2.0**11
FIRST_SCALE = 2.0**6
SECOND_SCALE = 2.0**-6
PARTIAL_SCALE = 2.0**7


def exchange(array, axes):
    return lax.all_to_all(array, axes, split_axis=0, concat_axis=0, tiled=True)


def pick(array, index, axis):
    return lax.dynamic_index_in_dim(
        array, index, axis=axis, keepdims=False, allow_negative_indices=False
    )


def pack(weight, moment_one, moment_two):
    high = lax.reduce_precision(weight, exponent_bits=5, mantissa_bits=10)
    rest = (weight - high) * REST_SCALE
    return jnp.stack((high, rest, moment_one * FIRST_SCALE, moment_two * SECOND_SCALE)).astype(
        jnp.float16
    )


def unpack(packed):
    wide = packed.astype(jnp.float32)
    return jnp.stack(
        (
            wide[:, 0] + wide[:, 1] * (1.0 / REST_SCALE),
            wide[:, 2] * (1.0 / FIRST_SCALE),
            wide[:, 3] * (1.0 / SECOND_SCALE),
        ),
        axis=1,
    )


def adam_update(weight, first_moment, second_moment, gradient):
    new_first = beta_first * first_moment + (1.0 - beta_first) * gradient
    new_second = beta_second * second_moment + (1.0 - beta_second) * gradient * gradient
    step_size = new_first / correct_first / (jnp.sqrt(new_second / correct_second) + 1e-08)
    new_weight = weight - learn_rate * (step_size + weight_decay * weight)
    return (new_weight, new_first, new_second)


def product_of(features, cotangents_ref):
    return lax.dot_general(
        features,
        cotangents_ref[...],
        (((0,), (0,)), ((), ())),
        preferred_element_type=jnp.float32,
    ).reshape(32, 8, 512)


def arrived_kernel(got_ref, cotangents_ref, out_ref):
    out_ref[...] = product_of(got_ref[...], cotangents_ref)


def own_kernel(mine_ref, tokens_ref, cotangents_ref, half_ref, out_ref, kept, arrived):
    mine = mine_ref[0]
    fetch = pltpu.make_async_copy(tokens_ref.at[:, mine], kept, arrived)
    fetch.start()
    out_ref[:, 1 - mine] = half_ref[...]
    fetch.wait()
    out_ref[:, mine] = product_of(kept[...].reshape(1792, 256), cotangents_ref)


def products(mine, tokens, got, cotangents):
    in_smem = pl.BlockSpec(memory_space=pltpu.SMEM)
    in_vmem = pl.BlockSpec(memory_space=pltpu.VMEM)
    in_any = pl.BlockSpec(memory_space=pl.ANY)
    shared = dict(
        out_specs=in_vmem,
        compiler_params=pltpu.CompilerParams(vmem_limit_bytes=40 * 1024 * 1024),
        cost_estimate=pl.CostEstimate(
            flops=2 * 1792 * 256 * 512, bytes_accessed=3 * 1024 * 1024, transcendentals=0
        ),
    )
    half = pl.pallas_call(
        arrived_kernel,
        out_shape=jax.ShapeDtypeStruct((32, 8, 512), jnp.float32),
        in_specs=[in_vmem, in_vmem],
        **shared,
    )(got, cotangents)
    return pl.pallas_call(
        own_kernel,
        out_shape=jax.ShapeDtypeStruct((32, 2, 8, 512), jnp.float32),
        in_specs=[in_smem, in_any, in_vmem, in_vmem],
        scratch_shapes=[
            pltpu.VMEM((16, 112, 256), jnp.bfloat16),
            pltpu.SemaphoreType.DMA,
        ],
        **shared,
    )(mine.reshape(1), tokens, cotangents, half)


def assemble_kernel(core_ref, half_ref, sibling_ref, *refs):
    outs, done = refs[:3], refs[3]
    core = core_ref[0]
    copies = []
    for i in range(3):
        for j, (source, place) in enumerate(((half_ref, core), (sibling_ref, 1 - core))):
            copies.append(
                pltpu.make_async_copy(source.at[:, i], outs[i].at[place], done.at[2 * i + j])
            )
    for copy in copies:
        copy.start()
    for copy in copies:
        copy.wait()


def assemble(core, half, sibling):
    in_vmem = pl.BlockSpec(memory_space=pltpu.VMEM)
    outs = pl.pallas_call(
        assemble_kernel,
        out_shape=[jax.ShapeDtypeStruct((2, 16, 8, 512), jnp.float32)] * 3,
        in_specs=[pl.BlockSpec(memory_space=pltpu.SMEM), in_vmem, in_vmem],
        out_specs=[pl.BlockSpec(memory_space=pl.ANY)] * 3,
        scratch_shapes=[pltpu.SemaphoreType.DMA((6,))],
        compiler_params=pltpu.CompilerParams(vmem_limit_bytes=40 * 1024 * 1024),
    )(core.reshape(1), half, sibling)
    return tuple(item.reshape(256, 512) for item in outs)


def on_device(activations, key_grads, partners, master_weight, first_moment, second_moment):
    mine = lax.axis_index("xh")
    other = 1 - mine
    core = lax.axis_index("c")
    column = lax.axis_index(("xl", "y"))

    def by_block(own, peer):
        return jnp.where(mine == 0, own, peer), jnp.where(mine == 0, peer, own)

    tokens = activations.reshape(16, 2, 112, 256)
    got = lax.ppermute(pick(tokens, other, 1), "xh", SWAP)

    first_row = 128 * core + 16 * column

    def eight(side):
        return jnp.stack(
            [
                lax.dynamic_slice_in_dim(
                    item, first_row + 8 * side, 8, axis=0, allow_negative_indices=False
                )
                for item in (master_weight, first_moment, second_moment)
            ]
        )

    scaled = (key_grads.astype(jnp.float32) * KEY_SCALE).astype(jnp.float16)
    cotangents = lax.all_gather(scaled, "z", axis=0, tiled=True)
    got, cotangents = lax.optimization_barrier((got, cotangents))
    own_rows = eight(mine)
    peer_rows = lax.ppermute(eight(other), "xh", SWAP)
    cotangents = (cotangents.astype(jnp.float32) * (1.0 / KEY_SCALE)).astype(jnp.bfloat16)

    partial = products(mine, tokens, got.reshape(1792, 256), cotangents)
    pieces = exchange((partial * PARTIAL_SCALE).astype(jnp.float16), PLANE)
    gradient = jnp.sum(pieces.astype(jnp.float32), axis=0) * (1.0 / PARTIAL_SCALE)

    old = jnp.stack(by_block(own_rows, peer_rows), axis=1)
    results = adam_update(old[0], old[1], old[2], gradient)

    along = lax.all_gather(pack(*results), "z", axis=0, tiled=False)
    here = 2 * lax.axis_index("z")

    def wanted(index):
        place = pick(partners, index, 0)
        return pick(pick(along, place >> 1, 0), place & 1, 1)

    placed = jnp.stack([wanted(here + i) for i in range(2)]).reshape(1, 2, 4, 8, 512)
    shared = jnp.broadcast_to(placed, (8, 2, 4, 8, 512)).reshape(16, 4, 8, 512)
    half = unpack(exchange(shared, CHIPS))
    sibling = lax.ppermute(half, "c", SWAP)
    return assemble(core, half, sibling)


def solution(mesh):
    names = tuple(name for name, _ in PARTS)
    sizes = tuple(size for _, size in PARTS)
    fine = Mesh(mesh.devices.reshape(sizes), names)
    return jax.shard_map(
        on_device,
        mesh=fine,
        in_specs=(
            P(DP, FSDP),
            P(DP + FSDP, None),
            P(),
            P(FSDP, None),
            P(FSDP, None),
            P(FSDP, None),
        ),
        out_specs=(P(FSDP, None), P(FSDP, None), P(FSDP, None)),
        check_vma=False,
    )
```

```python
import jax
import jax.numpy as jnp
from jax import lax
from jax.experimental import pallas as pl
from jax.experimental.pallas import tpu as pltpu
from jax.sharding import Mesh
from jax.sharding import PartitionSpec as P

beta_first = 0.9
beta_second = 0.95
learn_rate = 0.01
weight_decay = 0.1
correct_first = 1.0 - 0.9**10
correct_second = 1.0 - 0.95**10

PARTS = (("xl", 2), ("y", 4), ("c", 2), ("z", 16), ("xh", 2))
DP = ("xl", "y", "c")
FSDP = ("z", "xh")
CHIPS = ("xl", "y", "xh")
PLANE = ("xl", "y", "c", "xh")
SWAP = [(0, 1), (1, 0)]
KEY_SCALE = 2.0**21
REST_SCALE = 2.0**11
FIRST_SCALE = 2.0**6
SECOND_SCALE = 2.0**-6
PARTIAL_SCALE = 2.0**7


def exchange(array, axes):
    return lax.all_to_all(array, axes, split_axis=0, concat_axis=0, tiled=True)


def pick(array, index, axis):
    return lax.dynamic_index_in_dim(
        array, index, axis=axis, keepdims=False, allow_negative_indices=False
    )


def pack(weight, moment_one, moment_two):
    high = lax.reduce_precision(weight, exponent_bits=5, mantissa_bits=10)
    rest = (weight - high) * REST_SCALE
    return jnp.stack((high, rest, moment_one * FIRST_SCALE, moment_two * SECOND_SCALE)).astype(
        jnp.float16
    )


def unpack(packed):
    wide = packed.astype(jnp.float32)
    return jnp.stack(
        (
            wide[:, 0] + wide[:, 1] * (1.0 / REST_SCALE),
            wide[:, 2] * (1.0 / FIRST_SCALE),
            wide[:, 3] * (1.0 / SECOND_SCALE),
        ),
        axis=1,
    )


def adam_update(weight, first_moment, second_moment, gradient):
    new_first = beta_first * first_moment + (1.0 - beta_first) * gradient
    new_second = beta_second * second_moment + (1.0 - beta_second) * gradient * gradient
    step_size = new_first / correct_first / (jnp.sqrt(new_second / correct_second) + 1e-08)
    new_weight = weight - learn_rate * (step_size + weight_decay * weight)
    return (new_weight, new_first, new_second)


def products_kernel(mine_ref, tokens_ref, got_ref, cotangents_ref, out_ref, kept, arrived):
    mine = mine_ref[0]
    fetch = pltpu.make_async_copy(tokens_ref.at[:, mine], kept, arrived)
    fetch.start()

    def product(features):
        return lax.dot_general(
            features,
            cotangents_ref[...],
            (((0,), (0,)), ((), ())),
            preferred_element_type=jnp.float32,
        ).reshape(32, 8, 512)

    out_ref[:, 1 - mine] = product(got_ref[...])
    fetch.wait()
    out_ref[:, mine] = product(kept[...].reshape(1792, 256))


def products(mine, tokens, got, cotangents):
    in_vmem = pl.BlockSpec(memory_space=pltpu.VMEM)
    return pl.pallas_call(
        products_kernel,
        out_shape=jax.ShapeDtypeStruct((32, 2, 8, 512), jnp.float32),
        in_specs=[
            pl.BlockSpec(memory_space=pltpu.SMEM),
            pl.BlockSpec(memory_space=pl.ANY),
            in_vmem,
            in_vmem,
        ],
        out_specs=in_vmem,
        scratch_shapes=[
            pltpu.VMEM((16, 112, 256), jnp.bfloat16),
            pltpu.SemaphoreType.DMA,
        ],
        compiler_params=pltpu.CompilerParams(vmem_limit_bytes=40 * 1024 * 1024),
        cost_estimate=pl.CostEstimate(
            flops=2 * 2 * 1792 * 256 * 512, bytes_accessed=6 * 1024 * 1024, transcendentals=0
        ),
    )(mine.reshape(1), tokens, got, cotangents)


def assemble_kernel(core_ref, half_ref, sibling_ref, *refs):
    outs, done = refs[:3], refs[3]
    core = core_ref[0]
    copies = []
    for i in range(3):
        for j, (source, place) in enumerate(((half_ref, core), (sibling_ref, 1 - core))):
            copies.append(
                pltpu.make_async_copy(
                    source.at[:, :, i], outs[i].at[:, place], done.at[2 * i + j]
                )
            )
    for copy in copies:
        copy.start()
    for copy in copies:
        copy.wait()


def assemble(core, half, sibling):
    in_vmem = pl.BlockSpec(memory_space=pltpu.VMEM)
    outs = pl.pallas_call(
        assemble_kernel,
        out_shape=[jax.ShapeDtypeStruct((8, 2, 2, 8, 512), jnp.float32)] * 3,
        in_specs=[pl.BlockSpec(memory_space=pltpu.SMEM), in_vmem, in_vmem],
        out_specs=[pl.BlockSpec(memory_space=pl.ANY)] * 3,
        scratch_shapes=[pltpu.SemaphoreType.DMA((6,))],
        compiler_params=pltpu.CompilerParams(vmem_limit_bytes=40 * 1024 * 1024),
    )(core.reshape(1), half, sibling)
    return tuple(item.reshape(256, 512) for item in outs)


def on_device(activations, key_grads, partners, master_weight, first_moment, second_moment):
    mine = lax.axis_index("xh")
    other = 1 - mine
    core = lax.axis_index("c")
    column = lax.axis_index(("xl", "y"))

    def by_block(own, peer):
        return jnp.where(mine == 0, own, peer), jnp.where(mine == 0, peer, own)

    tokens = activations.reshape(16, 2, 112, 256)
    got = lax.ppermute(pick(tokens, other, 1), "xh", SWAP)

    first_row = 32 * column + 16 * core

    def eight(side):
        return jnp.stack(
            [
                lax.dynamic_slice_in_dim(
                    item, first_row + 8 * side, 8, axis=0, allow_negative_indices=False
                )
                for item in (master_weight, first_moment, second_moment)
            ]
        )

    scaled = (key_grads.astype(jnp.float32) * KEY_SCALE).astype(jnp.float16)
    cotangents = lax.all_gather(scaled, "z", axis=0, tiled=True)
    got, cotangents = lax.optimization_barrier((got, cotangents))
    own_rows = eight(mine)
    peer_rows = lax.ppermute(eight(other), "xh", SWAP)
    cotangents = (cotangents.astype(jnp.float32) * (1.0 / KEY_SCALE)).astype(jnp.bfloat16)

    partial = products(mine, tokens, got.reshape(1792, 256), cotangents)
    pieces = exchange((partial * PARTIAL_SCALE).astype(jnp.float16), PLANE)
    gradient = jnp.sum(pieces.astype(jnp.float32), axis=0) * (1.0 / PARTIAL_SCALE)

    old = jnp.stack(by_block(own_rows, peer_rows), axis=1)
    results = adam_update(old[0], old[1], old[2], gradient)

    along = lax.all_gather(pack(*results), "z", axis=0, tiled=False)
    here = 2 * lax.axis_index("z")

    def wanted(index):
        place = pick(partners, index, 0)
        return pick(pick(along, place >> 1, 0), place & 1, 1)

    placed = jnp.stack([wanted(here + i) for i in range(2)]).reshape(1, 2, 4, 8, 512)
    shared = jnp.broadcast_to(placed, (8, 2, 4, 8, 512)).reshape(16, 4, 8, 512)
    half = unpack(exchange(shared, CHIPS)).reshape(8, 2, 3, 8, 512)
    sibling = lax.ppermute(half, "c", SWAP)
    return assemble(core, half, sibling)


def solution(mesh):
    names = tuple(name for name, _ in PARTS)
    sizes = tuple(size for _, size in PARTS)
    fine = Mesh(mesh.devices.reshape(sizes), names)
    return jax.shard_map(
        on_device,
        mesh=fine,
        in_specs=(
            P(DP, FSDP),
            P(DP + FSDP, None),
            P(),
            P(FSDP, None),
            P(FSDP, None),
            P(FSDP, None),
        ),
        out_specs=(P(FSDP, None), P(FSDP, None), P(FSDP, None)),
        check_vma=False,
    )
```

```python
import jax
import jax.numpy as jnp
from jax import lax
from jax.experimental import pallas as pl
from jax.experimental.pallas import tpu as pltpu
from jax.sharding import Mesh
from jax.sharding import PartitionSpec as P

beta_first = 0.9
beta_second = 0.95
learn_rate = 0.01
weight_decay = 0.1
correct_first = 1.0 - 0.9**10
correct_second = 1.0 - 0.95**10

PARTS = (("xl", 2), ("y", 4), ("c", 2), ("z", 16), ("xh", 2))
DP = ("xl", "y", "c")
FSDP = ("z", "xh")
CHIPS = ("xl", "y", "xh")
PLANE = ("c", "xl", "y", "xh")
SWAP = [(0, 1), (1, 0)]
KEY_SCALE = 2.0**21
REST_SCALE = 2.0**11
FIRST_SCALE = 2.0**6
SECOND_SCALE = 2.0**-6
PARTIAL_SCALE = 2.0**7


def exchange(array, axes):
    return lax.all_to_all(array, axes, split_axis=0, concat_axis=0, tiled=True)


def pick(array, index, axis):
    return lax.dynamic_index_in_dim(
        array, index, axis=axis, keepdims=False, allow_negative_indices=False
    )


def pack(weight, moment_one, moment_two):
    high = lax.reduce_precision(weight, exponent_bits=5, mantissa_bits=10)
    rest = (weight - high) * REST_SCALE
    return jnp.stack((high, rest, moment_one * FIRST_SCALE, moment_two * SECOND_SCALE)).astype(
        jnp.float16
    )


def unpack(packed):
    wide = packed.astype(jnp.float32)
    return jnp.stack(
        (
            wide[:, 0] + wide[:, 1] * (1.0 / REST_SCALE),
            wide[:, 2] * (1.0 / FIRST_SCALE),
            wide[:, 3] * (1.0 / SECOND_SCALE),
        ),
        axis=1,
    )


def adam_update(weight, first_moment, second_moment, gradient):
    new_first = beta_first * first_moment + (1.0 - beta_first) * gradient
    new_second = beta_second * second_moment + (1.0 - beta_second) * gradient * gradient
    step_size = new_first / correct_first / (jnp.sqrt(new_second / correct_second) + 1e-08)
    new_weight = weight - learn_rate * (step_size + weight_decay * weight)
    return (new_weight, new_first, new_second)


def products_kernel(mine_ref, tokens_ref, got_ref, cotangents_ref, out_ref, kept, arrived):
    mine = mine_ref[0]
    fetch = pltpu.make_async_copy(tokens_ref.at[:, mine], kept, arrived)
    fetch.start()

    def product(features):
        return lax.dot_general(
            features,
            cotangents_ref[...],
            (((0,), (0,)), ((), ())),
            preferred_element_type=jnp.float32,
        ).reshape(32, 8, 512)

    out_ref[:, 1 - mine] = product(got_ref[...])
    fetch.wait()
    out_ref[:, mine] = product(kept[...].reshape(1792, 256))


def products(mine, tokens, got, cotangents):
    in_vmem = pl.BlockSpec(memory_space=pltpu.VMEM)
    return pl.pallas_call(
        products_kernel,
        out_shape=jax.ShapeDtypeStruct((32, 2, 8, 512), jnp.float32),
        in_specs=[
            pl.BlockSpec(memory_space=pltpu.SMEM),
            pl.BlockSpec(memory_space=pl.ANY),
            in_vmem,
            in_vmem,
        ],
        out_specs=in_vmem,
        scratch_shapes=[
            pltpu.VMEM((16, 112, 256), jnp.bfloat16),
            pltpu.SemaphoreType.DMA,
        ],
        compiler_params=pltpu.CompilerParams(vmem_limit_bytes=40 * 1024 * 1024),
        cost_estimate=pl.CostEstimate(
            flops=2 * 2 * 1792 * 256 * 512, bytes_accessed=6 * 1024 * 1024, transcendentals=0
        ),
    )(mine.reshape(1), tokens, got, cotangents)


def assemble_kernel(core_ref, half_ref, sibling_ref, *refs):
    outs, done = refs[:3], refs[3]
    core = core_ref[0]
    copies = []
    for i in range(3):
        for j, (source, place) in enumerate(((half_ref, core), (sibling_ref, 1 - core))):
            copies.append(
                pltpu.make_async_copy(source.at[:, i], outs[i].at[place], done.at[2 * i + j])
            )
    for copy in copies:
        copy.start()
    for copy in copies:
        copy.wait()


def assemble(core, half, sibling):
    in_vmem = pl.BlockSpec(memory_space=pltpu.VMEM)
    outs = pl.pallas_call(
        assemble_kernel,
        out_shape=[jax.ShapeDtypeStruct((2, 16, 8, 512), jnp.float32)] * 3,
        in_specs=[pl.BlockSpec(memory_space=pltpu.SMEM), in_vmem, in_vmem],
        out_specs=[pl.BlockSpec(memory_space=pl.ANY)] * 3,
        scratch_shapes=[pltpu.SemaphoreType.DMA((6,))],
        compiler_params=pltpu.CompilerParams(vmem_limit_bytes=40 * 1024 * 1024),
    )(core.reshape(1), half, sibling)
    return tuple(item.reshape(256, 512) for item in outs)


def on_device(activations, key_grads, partners, master_weight, first_moment, second_moment):
    mine = lax.axis_index("xh")
    other = 1 - mine
    core = lax.axis_index("c")
    column = lax.axis_index(("xl", "y"))

    def by_block(own, peer):
        return jnp.where(mine == 0, own, peer), jnp.where(mine == 0, peer, own)

    tokens = activations.reshape(16, 2, 112, 256)
    got = lax.ppermute(pick(tokens, other, 1), "xh", SWAP)

    first_row = 128 * core + 16 * column

    def eight(side):
        return jnp.stack(
            [
                lax.dynamic_slice_in_dim(
                    item, first_row + 8 * side, 8, axis=0, allow_negative_indices=False
                )
                for item in (master_weight, first_moment, second_moment)
            ]
        )

    scaled = (key_grads.astype(jnp.float32) * KEY_SCALE).astype(jnp.float16)
    cotangents = lax.all_gather(scaled, "z", axis=0, tiled=True)
    got, cotangents = lax.optimization_barrier((got, cotangents))
    own_rows = eight(mine)
    peer_rows = lax.ppermute(eight(other), "xh", SWAP)
    cotangents = (cotangents.astype(jnp.float32) * (1.0 / KEY_SCALE)).astype(jnp.bfloat16)

    partial = products(mine, tokens, got.reshape(1792, 256), cotangents)
    pieces = exchange((partial * PARTIAL_SCALE).astype(jnp.float16), PLANE)
    gradient = jnp.sum(pieces.astype(jnp.float32), axis=0) * (1.0 / PARTIAL_SCALE)

    old = jnp.stack(by_block(own_rows, peer_rows), axis=1)
    results = adam_update(old[0], old[1], old[2], gradient)

    along = lax.all_gather(pack(*results), "z", axis=0, tiled=False)
    here = 2 * lax.axis_index("z")

    def wanted(index):
        place = pick(partners, index, 0)
        return pick(pick(along, place >> 1, 0), place & 1, 1)

    placed = jnp.stack([wanted(here + i) for i in range(2)]).reshape(1, 2, 4, 8, 512)
    shared = jnp.broadcast_to(placed, (8, 2, 4, 8, 512)).reshape(16, 4, 8, 512)
    packed = exchange(shared, CHIPS)
    sibling = lax.ppermute(packed, "c", SWAP)
    return assemble(core, unpack(packed), unpack(sibling))


def solution(mesh):
    names = tuple(name for name, _ in PARTS)
    sizes = tuple(size for _, size in PARTS)
    fine = Mesh(mesh.devices.reshape(sizes), names)
    return jax.shard_map(
        on_device,
        mesh=fine,
        in_specs=(
            P(DP, FSDP),
            P(DP + FSDP, None),
            P(),
            P(FSDP, None),
            P(FSDP, None),
            P(FSDP, None),
        ),
        out_specs=(P(FSDP, None), P(FSDP, None), P(FSDP, None)),
        check_vma=False,
    )
```

```python
import jax
import jax.numpy as jnp
from jax import lax
from jax.experimental import pallas as pl
from jax.experimental.pallas import tpu as pltpu
from jax.sharding import Mesh
from jax.sharding import PartitionSpec as P

beta_first = 0.9
beta_second = 0.95
learn_rate = 0.01
weight_decay = 0.1
correct_first = 1.0 - 0.9**10
correct_second = 1.0 - 0.95**10

PARTS = (("xl", 2), ("y", 4), ("c", 2), ("z", 16), ("xh", 2))
DP = ("xl", "y", "c")
FSDP = ("z", "xh")
CHIPS = ("xl", "y", "xh")
PLANE = ("c", "xl", "y", "xh")
SWAP = [(0, 1), (1, 0)]
KEY_SCALE = 2.0**21
REST_SCALE = 2.0**11
FIRST_SCALE = 2.0**6
SECOND_SCALE = 2.0**-6
PARTIAL_SCALE = 2.0**7


def exchange(array, axes):
    return lax.all_to_all(array, axes, split_axis=0, concat_axis=0, tiled=True)


def pick(array, index, axis):
    return lax.dynamic_index_in_dim(
        array, index, axis=axis, keepdims=False, allow_negative_indices=False
    )


def pack(weight, moment_one, moment_two):
    high = lax.reduce_precision(weight, exponent_bits=5, mantissa_bits=10)
    rest = (weight - high) * REST_SCALE
    return jnp.stack((high, rest, moment_one * FIRST_SCALE, moment_two * SECOND_SCALE)).astype(
        jnp.float16
    )


def unpack(packed):
    wide = packed.astype(jnp.float32)
    return jnp.stack(
        (
            wide[:, 0] + wide[:, 1] * (1.0 / REST_SCALE),
            wide[:, 2] * (1.0 / FIRST_SCALE),
            wide[:, 3] * (1.0 / SECOND_SCALE),
        ),
        axis=1,
    )


def adam_update(weight, first_moment, second_moment, gradient):
    new_first = beta_first * first_moment + (1.0 - beta_first) * gradient
    new_second = beta_second * second_moment + (1.0 - beta_second) * gradient * gradient
    step_size = new_first / correct_first / (jnp.sqrt(new_second / correct_second) + 1e-08)
    new_weight = weight - learn_rate * (step_size + weight_decay * weight)
    return (new_weight, new_first, new_second)


def products_kernel(mine_ref, tokens_ref, got_ref, cotangents_ref, out_ref, kept, arrived):
    mine = mine_ref[0]
    fetch = pltpu.make_async_copy(tokens_ref.at[:, mine], kept, arrived)
    fetch.start()

    def product(features):
        return lax.dot_general(
            features,
            cotangents_ref[...],
            (((0,), (0,)), ((), ())),
            preferred_element_type=jnp.float32,
        ).reshape(32, 8, 512)

    out_ref[:, 1 - mine] = product(got_ref[...])
    fetch.wait()
    out_ref[:, mine] = product(kept[...].reshape(1792, 256))


def products(mine, tokens, got, cotangents):
    in_vmem = pl.BlockSpec(memory_space=pltpu.VMEM)
    return pl.pallas_call(
        products_kernel,
        out_shape=jax.ShapeDtypeStruct((32, 2, 8, 512), jnp.float32),
        in_specs=[
            pl.BlockSpec(memory_space=pltpu.SMEM),
            pl.BlockSpec(memory_space=pl.ANY),
            in_vmem,
            in_vmem,
        ],
        out_specs=in_vmem,
        scratch_shapes=[
            pltpu.VMEM((16, 112, 256), jnp.bfloat16),
            pltpu.SemaphoreType.DMA,
        ],
        compiler_params=pltpu.CompilerParams(vmem_limit_bytes=40 * 1024 * 1024),
        cost_estimate=pl.CostEstimate(
            flops=2 * 2 * 1792 * 256 * 512, bytes_accessed=6 * 1024 * 1024, transcendentals=0
        ),
    )(mine.reshape(1), tokens, got, cotangents)


def place_kernel(where_ref, source_ref, *refs):
    outs, done = refs[-4:-1], refs[-1]
    half = where_ref[0]
    copies = [
        pltpu.make_async_copy(source_ref.at[:, i], outs[i].at[half], done.at[i])
        for i in range(3)
    ]
    for copy in copies:
        copy.start()
    for copy in copies:
        copy.wait()


def place(half, source, outs=()):
    return pl.pallas_call(
        place_kernel,
        out_shape=[jax.ShapeDtypeStruct((2, 16, 8, 512), jnp.float32)] * 3,
        in_specs=[
            pl.BlockSpec(memory_space=pltpu.SMEM),
            pl.BlockSpec(memory_space=pltpu.VMEM),
        ]
        + [pl.BlockSpec(memory_space=pltpu.HBM)] * len(outs),
        out_specs=[pl.BlockSpec(memory_space=pltpu.HBM)] * 3,
        input_output_aliases={2 + i: i for i in range(len(outs))},
        scratch_shapes=[pltpu.SemaphoreType.DMA((3,))],
        compiler_params=pltpu.CompilerParams(vmem_limit_bytes=40 * 1024 * 1024),
        cost_estimate=pl.CostEstimate(
            flops=0, bytes_accessed=2 * 1024 * 1024, transcendentals=0
        ),
    )(half.reshape(1), source, *outs)


def on_device(activations, key_grads, partners, master_weight, first_moment, second_moment):
    mine = lax.axis_index("xh")
    other = 1 - mine
    core = lax.axis_index("c")
    column = lax.axis_index(("xl", "y"))

    def by_block(own, peer):
        return jnp.where(mine == 0, own, peer), jnp.where(mine == 0, peer, own)

    tokens = activations.reshape(16, 2, 112, 256)
    got = lax.ppermute(pick(tokens, other, 1), "xh", SWAP)

    first_row = 128 * core + 16 * column

    def eight(side):
        return jnp.stack(
            [
                lax.dynamic_slice_in_dim(
                    item, first_row + 8 * side, 8, axis=0, allow_negative_indices=False
                )
                for item in (master_weight, first_moment, second_moment)
            ]
        )

    scaled = (key_grads.astype(jnp.float32) * KEY_SCALE).astype(jnp.float16)
    cotangents = lax.all_gather(scaled, "z", axis=0, tiled=True)
    got, cotangents = lax.optimization_barrier((got, cotangents))
    own_rows = eight(mine)
    peer_rows = lax.ppermute(eight(other), "xh", SWAP)
    cotangents = (cotangents.astype(jnp.float32) * (1.0 / KEY_SCALE)).astype(jnp.bfloat16)

    partial = products(mine, tokens, got.reshape(1792, 256), cotangents)
    pieces = exchange((partial * PARTIAL_SCALE).astype(jnp.float16), PLANE)
    gradient = jnp.sum(pieces.astype(jnp.float32), axis=0) * (1.0 / PARTIAL_SCALE)

    old = jnp.stack(by_block(own_rows, peer_rows), axis=1)
    results = adam_update(old[0], old[1], old[2], gradient)

    along = lax.all_gather(pack(*results), "z", axis=0, tiled=False)
    here = 2 * lax.axis_index("z")

    def wanted(index):
        place = pick(partners, index, 0)
        return pick(pick(along, place >> 1, 0), place & 1, 1)

    placed = jnp.stack([wanted(here + i) for i in range(2)]).reshape(1, 2, 4, 8, 512)
    shared = jnp.broadcast_to(placed, (8, 2, 4, 8, 512)).reshape(16, 4, 8, 512)
    packed = exchange(shared, CHIPS)
    sibling = lax.ppermute(packed, "c", SWAP)
    outs = place(1 - core, unpack(sibling), place(core, unpack(packed)))
    return tuple(item.reshape(256, 512) for item in outs)


def solution(mesh):
    names = tuple(name for name, _ in PARTS)
    sizes = tuple(size for _, size in PARTS)
    fine = Mesh(mesh.devices.reshape(sizes), names)
    return jax.shard_map(
        on_device,
        mesh=fine,
        in_specs=(
            P(DP, FSDP),
            P(DP + FSDP, None),
            P(),
            P(FSDP, None),
            P(FSDP, None),
            P(FSDP, None),
        ),
        out_specs=(P(FSDP, None), P(FSDP, None), P(FSDP, None)),
        check_vma=False,
    )
```
